32 devices in a mesh: px: 16 (over z, y, x), py: 2 (over core).
Axes of the slice: x: 2, y: 2, z: 4, core: 2. Of those that a mesh axis runs over, the one named last changes fastest.
Arguments:
- levels: int32 [256, 2048], P('px', 'py'), may hold values from 0 to 15
- conv_table: bfloat16 [64, 144], replicated, may hold values from -2 to 2
- conv_bias: float32 [64], replicated, may hold values from -3 to 3
- mix_weight: bfloat16 [64, 64], replicated, may hold values from -0.75 to 0.75
- mix_bias: float32 [64], replicated, may hold values from -3 to 3
- decoder: bfloat16 [5, 40, 64], replicated, may hold values from -0.15625 to 0.15625
- green_rows: float32 [8, 2, 64, 256], P(None, None, None, 'px'), may hold values from -0.375 to 0.375
- green_cols: float32 [8, 2, 64, 2048], P(None, None, None, 'py'), may hold values from -0.125 to 0.125
- focal_order: int32 [64], replicated, may hold values from 0 to 63, each once
Outputs:
- focal: float32 [8, 64, 512], P('py', 'px')
The draws below stay inside these ranges and needn't reach their ends.
Inputs may be any that keep to these rules, and one draw needn't show every extreme that they name: `focal_order`: each of the 64 focal rows appears exactly once.
All inputs are finite; a program needn't handle non-finite values.
Results may differ from the reference program's by a relative error of at most 0.0045.
Values sent between devices are 32-bit elements; how exact they have to be, the bound alone decides.
A program may use at most 128 MiB of HBM per device.

```python
import jax
import jax.numpy as jnp
from jax import lax

R_DEV = 16
HID = 64
LEVELS = 16
CH = 8
M = 2
KS = 5
Z = 8
U = 64
V = 64
NXA = 256
NYA = 2048
N_PX = 16


def set_ends(array, rng, least, top_value):
    index_at = [jax.random.randint(jax.random.fold_in(rng, axis), (), 0, length) for axis, length in enumerate(array.shape)]
    widest = array.shape.index(max(array.shape))
    neighbour = index_at[:widest] + [(index_at[widest] + 1) % array.shape[widest]] + index_at[widest + 1:]
    return array.at[tuple(index_at)].set(least).at[tuple(neighbour)].set(top_value)


def shard_levels(stream_key, dims, cuts, least, largest):
    def one(dim, blocks):
        steps = jax.random.uniform(jax.random.fold_in(jax.random.fold_in(stream_key, 6), dim), (blocks,), jnp.float32, least / len(cuts), largest / len(cuts))
        return jnp.repeat(jnp.exp(steps), dims[dim] // blocks).reshape((-1,) + (1,) * (len(dims) - dim - 1))

    factor_of = one(*cuts[0])
    for cut in cuts[1:]:
        factor_of = factor_of * one(*cut)
    return factor_of


def noise(rng, shape, deviation, bound, split=(), kind=jnp.bfloat16):
    factor_of = shard_levels(rng, shape, split, -0.22, 0.18) if split else 1.0
    entries = jax.random.normal(rng, shape, jnp.float32) * deviation * factor_of
    return jnp.minimum(jnp.maximum(entries, -bound), bound).astype(kind)


def setup_inputs(seed: int = 0) -> dict:
    arg_keys = jax.random.split(jax.random.key(seed), 10)
    levels = set_ends(jax.random.randint(arg_keys[0], (NXA, NYA), 0, LEVELS), jax.random.fold_in(arg_keys[0], 1), 0, LEVELS - 1).astype(jnp.int32)
    conv_table = noise(arg_keys[1], (HID, 9 * LEVELS), 9 ** -0.5, 2.0)
    conv_bias = noise(arg_keys[2], (HID,), 0.5, 3.0, (), jnp.float32)
    mix_weight = noise(arg_keys[3], (HID, HID), HID ** -0.5, 0.75)
    mix_bias = noise(arg_keys[4], (HID,), 0.5, 3.0, (), jnp.float32)
    decoder = noise(arg_keys[5], (KS, KS * CH, HID), (KS * KS * HID) ** -0.5, 0.15625)
    green_rows = noise(arg_keys[6], (Z, 2, U, NXA), NXA ** -0.5, 0.375, ((3, 16),), jnp.float32)
    green_cols = noise(arg_keys[7], (Z, 2, V, NYA), NYA ** -0.5, 0.125, ((3, 2),), jnp.float32)
    focal_order = jax.random.permutation(arg_keys[8], U).astype(jnp.int32)
    return dict(levels=levels, conv_table=conv_table, conv_bias=conv_bias, mix_weight=mix_weight, mix_bias=mix_bias, decoder=decoder, green_rows=green_rows, green_cols=green_cols, focal_order=focal_order)


exact_prec = lax.Precision.HIGHEST


def level_features(levels_ext, valid_ext, rows_out, cols_out, conv_table, conv_bias, mix_weight, mix_bias):
    count_levels = conv_table.shape[1] // 9
    level_ids = jnp.arange(count_levels, dtype=jnp.int32)[:, None, None]
    stacks = []
    for row_tap in range(3):
        for col_tap in range(3):
            window = levels_ext[row_tap:row_tap + rows_out, col_tap:col_tap + cols_out]
            inside = valid_ext[row_tap:row_tap + rows_out, col_tap:col_tap + cols_out]
            match_map = (window[None] == level_ids).astype(jnp.float32) * inside[None]
            stacks.append(match_map.astype(jnp.bfloat16))
    onehot = jnp.concatenate(stacks, axis=0).reshape(9 * count_levels, rows_out * cols_out)
    pre_act = jnp.dot(conv_table, onehot, preferred_element_type=jnp.float32) + conv_bias[:, None]
    hidden = jax.nn.gelu(pre_act).astype(jnp.bfloat16)
    mix_act = jnp.dot(mix_weight, hidden, preferred_element_type=jnp.float32) + mix_bias[:, None]
    center = valid_ext[1:1 + rows_out, 1:1 + cols_out].reshape(1, rows_out * cols_out)
    return (jax.nn.gelu(mix_act) * center).astype(jnp.bfloat16)


def focal_plane(product):
    real_part = product[0, 0] - product[1, 1]
    imag_part = product[0, 1] + product[1, 0]
    joined = jnp.stack([real_part, imag_part], axis=1)
    return joined.reshape(joined.shape[0], -1)


def reference(levels, conv_table, conv_bias, mix_weight, mix_bias, decoder, green_rows, green_cols, focal_order):
    total_cols = levels.shape[1]
    border = M + 1
    half = CH // 2
    levels_pad = jnp.pad(levels, border)
    valid_pad = jnp.pad(jnp.ones(levels.shape, jnp.float32), border)
    ordered = jnp.take(green_rows, focal_order, axis=2)
    blocks = ordered.reshape(Z, 2, U, N_PX, R_DEV).transpose(3, 0, 1, 2, 4)
    rows_out = R_DEV + 2 * M
    cols_out = total_cols + 2 * M

    def scan_step(running, inputs):
        block_id, gblock = inputs
        first_row = (block_id * R_DEV).astype(jnp.int32)
        levels_blk = lax.dynamic_slice_in_dim(levels_pad, first_row, R_DEV + 2 * border, 0)
        valid_blk = lax.dynamic_slice_in_dim(valid_pad, first_row, R_DEV + 2 * border, 0)
        features = level_features(levels_blk, valid_blk, rows_out, cols_out, conv_table, conv_bias, mix_weight, mix_bias)
        near_field = jnp.zeros((CH, R_DEV, total_cols), jnp.float32)
        for row_tap in range(KS):
            tap_block = jnp.dot(decoder[row_tap], features, preferred_element_type=jnp.float32).reshape(KS, CH, rows_out, cols_out)
            for col_tap in range(KS):
                near_field = near_field + tap_block[col_tap, :, 2 * M - row_tap:2 * M - row_tap + R_DEV, 2 * M - col_tap:2 * M - col_tap + total_cols]
        partial_value = jnp.einsum('zkur,hrc->zkuhc', gblock, near_field, precision=exact_prec)
        real_part = partial_value[:, 0, :, :half] - partial_value[:, 1, :, half:]
        imag_part = partial_value[:, 0, :, half:] + partial_value[:, 1, :, :half]
        return running + jnp.stack([real_part, imag_part], axis=1), None

    initial = jnp.zeros((Z, 2, U, half, total_cols), jnp.float32)
    aperture_sum, _ = lax.scan(scan_step, initial, (jnp.arange(N_PX, dtype=jnp.int32), blocks))
    planes = []
    for plane_id in range(Z):
        product = jnp.einsum('jvc,iupc->jiupv', green_cols[plane_id], aperture_sum[plane_id], precision=exact_prec)
        planes.append(focal_plane(product))
    return jnp.stack(planes, axis=0)
```

```python
import functools

import jax
import jax.numpy as jnp
from jax import lax
from jax.experimental import pallas as pl
from jax.experimental.pallas import tpu as pltpu
from jax.sharding import PartitionSpec as P

CH = 8
M = 2
KS = 5
Z = 8
U = 64
V = 64
LEVELS = 16
HID = 64
LANE = 128
MESH = pl.DeviceIdType.MESH
F32 = jnp.float32
BF16 = jnp.bfloat16


def gelu(x):
    inner = x * (0.7978845608028654 + (0.7978845608028654 * 0.044715) * (x * x))
    half = 0.5 * x
    return half + half * jnp.tanh(inner)


def column(row):
    n = row.shape[1]
    here = lax.broadcasted_iota(jnp.int32, (n, n), 0) == lax.broadcasted_iota(jnp.int32, (n, n), 1)
    return jnp.sum(jnp.where(here, row, 0.0), axis=1, keepdims=True)


def nt_dot(a, b):
    return lax.dot_general(a, b, (((1,), (1,)), ((), ())), preferred_element_type=F32)


def kernel(
    npx, npy, scatter,
    lv, table, conv_bias, mix, mix_bias, dec, rows_in, cols_in, order, out,
    lvx, lv_right, lv_left, lvr, onehot, w1, w2, wd, taps, cols, cols_right, cols_left, colsb,
    rows_up, rows_down, lhs, rhs, field, r0, a0, r1a, r1b, a1a, a1b, r2a, r2b, a2, r3,
    send, recv, rs_send, rs_recv, load_sem,
):
    px = lax.axis_index("px")
    py = lax.axis_index("py")
    ncols = lv.shape[1]
    wide = ncols + LANE
    nrows = lv.shape[0]
    ext = nrows + 2 * M

    up, down = lax.rem(px + npx - 1, npx), lax.rem(px + 1, npx)
    left, right = lax.rem(py + npy - 1, npy), lax.rem(py + 1, npy)
    near = [(up, py), (down, py), (px, left), (px, right), (up, left), (up, right), (down, left), (down, right)]
    greeted = list(near)
    if scatter:
        xq = lax.rem(px, 2)
        yq = lax.rem(px // 2, 2)
        zq = px // 4
        xdev = (px + 1 - 2 * xq, py)
        ydev = (px + 2 - 4 * yq, py)
        zdevs = [(lax.rem(px + 4 * d, 16), py) for d in (1, 2, 3)]
        greeted += [xdev, ydev] + zdevs

    load = pltpu.make_async_copy(cols_in, cols, load_sem)
    load.start()
    barrier = pltpu.get_barrier_semaphore()
    for device in greeted:
        pl.semaphore_signal(barrier, inc=1, device_id=device, device_id_type=MESH)

    w1[...] = jnp.zeros_like(w1)
    for r in range(2):
        w1[HID * r : HID * (r + 1), 48 * r : 48 * r + 144] = table[...].astype(F32)
    w2[...] = jnp.zeros_like(w2)
    for r in range(4):
        w2[HID * r : HID * (r + 1), HID * r : HID * (r + 1)] = mix[...].astype(F32)
    wd[...] = jnp.zeros_like(wd)
    for r in range(4):
        for t in range(KS):
            e = r + t
            wd[40 * e : 40 * (e + 1), HID * r : HID * (r + 1)] = dec[t].astype(F32)
    w1b = w1[...].astype(BF16)
    w2b = w2[...].astype(BF16)
    wdb = wd[...].astype(BF16)
    bias1 = column(conv_bias[...])
    bias1 = jnp.concatenate([bias1, bias1], axis=0)
    bias2 = column(mix_bias[...])
    bias2 = jnp.concatenate([bias2] * 4, axis=0)

    pl.semaphore_wait(barrier, len(greeted))

    def remote(slot, src, dst, device):
        copy = pltpu.make_async_remote_copy(
            src_ref=src, dst_ref=dst, send_sem=send.at[slot], recv_sem=recv.at[slot],
            device_id=device, device_id_type=MESH,
        )
        copy.start()
        return copy

    last = ncols - LANE
    level_copies = [
        remote(0, lv.at[nrows - 8 : nrows, :], lvx.at[0:8, :], (down, py)),
        remote(1, lv.at[0:8, :], lvx.at[8:16, :], (up, py)),
        remote(2, lv.at[:, 0:LANE], lv_right.at[8:24, :], (px, left)),
        remote(3, lv.at[:, last:ncols], lv_left.at[8:24, :], (px, right)),
        remote(4, lv.at[nrows - 8 : nrows, 0:LANE], lv_right.at[0:8, :], (down, left)),
        remote(5, lv.at[nrows - 8 : nrows, last:ncols], lv_left.at[0:8, :], (down, right)),
        remote(6, lv.at[0:8, 0:LANE], lv_right.at[24:32, :], (up, left)),
        remote(7, lv.at[0:8, last:ncols], lv_left.at[24:32, :], (up, right)),
    ]
    green_copies = [
        remote(8, rows_in, rows_up, (down, py)),
        remote(9, rows_in, rows_down, (up, py)),
        remote(10, cols_in.at[:, 0:LANE], cols_right, (px, left)),
        remote(11, cols_in.at[:, last:ncols], cols_left, (px, right)),
    ]
    for copy in level_copies:
        copy.wait()

    first_up, last_down = px == 0, px == npx - 1
    first_left, last_right = py == 0, py == npy - 1
    lane = lax.broadcasted_iota(jnp.int32, (32, LANE), 1)
    sub = lax.broadcasted_iota(jnp.int32, (32, LANE), 0)
    side = jnp.where(
        lane < 64,
        jnp.where(last_right, -1, lv_right[...]),
        jnp.where(first_left, -1, lv_left[...]),
    )
    side = jnp.where((sub < 8) & first_up, -1, side)
    side = jnp.where((sub >= 24) & last_down, -1, side)
    body = jnp.concatenate(
        [
            jnp.where(first_up, -1, lvx[0:8, :]),
            lv[...],
            jnp.where(last_down, -1, lvx[8:16, :]),
        ],
        axis=0,
    )
    whole = jnp.concatenate([body, side], axis=1)
    lvr[0] = pltpu.roll(whole, 1, 1)[:, :ncols]
    lvr[1] = body
    lvr[2] = pltpu.roll(whole, wide - 1, 1)[:, :ncols]
    ids = lax.broadcasted_iota(jnp.int32, (LEVELS, ncols), 0)
    for i in range(nrows + 2):
        for b in range(3):
            row = lvr[b, 7 + i : 8 + i, :]
            match = jnp.where(ids == row, 1.0, 0.0).astype(BF16)
            onehot[(3 * i + b) * LEVELS : (3 * i + b + 1) * LEVELS, :] = match

    for g in range(nrows // 4):
        parts = []
        for r in range(2):
            first = 96 * (2 * g + r)
            act = jnp.dot(w1b, onehot[first : first + 192, :], preferred_element_type=F32) + bias1
            parts.append(gelu(act).astype(BF16))
        hidden = jnp.concatenate(parts, axis=0)
        act = jnp.dot(w2b, hidden, preferred_element_type=F32) + bias2
        features = gelu(act).astype(BF16)
        tap = jnp.dot(wdb, features, preferred_element_type=F32)
        at = 160 * g
        if g == 0:
            taps[0:320, :] = tap
        else:
            taps[at : at + 160, :] += tap[0:160]
            taps[at + 160 : at + 320, :] = tap[160:320]

    blank = jnp.zeros((CH, LANE), F32)
    tiles = []
    for e in range(ext):
        total = None
        for s in range(KS):
            piece = jnp.concatenate([taps[40 * e + 8 * s : 40 * e + 8 * s + 8, :], blank], axis=1)
            if s != M:
                piece = pltpu.roll(piece, (s - M) % wide, 1)
            total = piece if total is None else total + piece
        tiles.append(total)
    near_field = jnp.concatenate(tiles, axis=0).astype(BF16)
    pr = lax.broadcasted_iota(jnp.int32, (CH * 32, CH * ext), 0)
    pc = lax.broadcasted_iota(jnp.int32, (CH * 32, CH * ext), 1)
    perm = jnp.where((pr // 32 == pc % 8) & ((pc // 8 + 30) % 32 == pr % 32), 1.0, 0.0).astype(BF16)
    near_field = jnp.dot(perm, near_field, preferred_element_type=F32).astype(BF16)

    for copy in green_copies:
        copy.wait()
    load.wait()
    colsb[:, 0:ncols] = cols[...].astype(BF16)
    clane = lax.broadcasted_iota(jnp.int32, cols_right.shape, 1)
    colsb[:, ncols:wide] = jnp.where(
        clane < 64,
        jnp.where(last_right, 0.0, cols_right[...]),
        jnp.where(first_left, 0.0, cols_left[...]),
    ).astype(BF16)

    share = U // npx
    height = U * Z
    er = lax.broadcasted_iota(jnp.int32, (height, U), 0)
    ec = lax.broadcasted_iota(jnp.int32, (height, U), 1)
    pick = jnp.where((er // (share * Z)) * share + er % share == ec, 1.0, 0.0).astype(BF16)
    wr = lax.broadcasted_iota(jnp.int32, (U, U), 0)
    placed = jnp.where(wr == order[...], 1.0, 0.0).astype(BF16)
    pick = nt_dot(pick, placed).astype(BF16)
    rlane = lax.broadcasted_iota(jnp.int32, rows_in.shape, 1)
    mixed = jnp.where(
        rlane % 16 < 8,
        jnp.where(last_down, 0.0, rows_down[...]),
        jnp.where(first_up, 0.0, rows_up[...]),
    )
    zr = (lax.broadcasted_iota(jnp.int32, (height, 256), 0) // share) % Z
    zc = lax.broadcasted_iota(jnp.int32, (height, 256), 1) // 32
    for source, value in enumerate((rows_in[...], mixed)):
        chosen = jnp.dot(pick, value.astype(BF16), preferred_element_type=F32)
        lhs[:, 256 * source : 256 * (source + 1)] = jnp.where(zr == zc, chosen, 0.0).astype(BF16)

    sums = nt_dot(near_field, colsb[...])
    sign = jnp.where(lax.broadcasted_iota(jnp.int32, (32, LANE), 1) < 64, -1.0, 1.0)
    for z in range(Z):
        for p in range(CH // 2):
            one = sums[32 * p : 32 * p + 32, LANE * z : LANE * (z + 1)]
            two = sums[32 * p + 128 : 32 * p + 160, LANE * z : LANE * (z + 1)]
            first = (one + sign * pltpu.roll(two, 64, 1)).astype(BF16)
            second = (sign * pltpu.roll(one, 64, 1) - two).astype(BF16)
            at = slice(LANE * p, LANE * (p + 1))
            for source in range(2):
                base = 256 * source + 32 * z
                rhs[base : base + 16, at] = first[16 * source : 16 * source + 16]
                rhs[base + 16 : base + 32, at] = second[16 * source : 16 * source + 16]
    product = jnp.dot(lhs[...], rhs[...], preferred_element_type=F32)
    if not scatter:
        out[...] = product
        return

    field[...] = product.reshape(field.shape)

    def exchange(slot, src, dst, device):
        copy = pltpu.make_async_remote_copy(
            src_ref=src, dst_ref=dst, send_sem=rs_send.at[slot], recv_sem=rs_recv.at[slot],
            device_id=device, device_id_type=MESH,
        )
        copy.start()
        return copy

    mine = pl.multiple_of(py * 16, 16)
    other = pl.multiple_of((1 - py) * 16, 16)
    core = exchange(0, field.at[:, :, :, pl.ds(other, 16), :], r0, (px, 1 - py))
    core.wait()
    a0[...] = field[:, :, :, pl.ds(mine, 16), :] + r0[...]
    half = a0.shape[-1] // 2
    ca = exchange(1, a0.at[:, :, 1 - xq, :, 0:half], r1a, xdev)
    cb = exchange(2, a0.at[:, 1 - yq, :, :, half : 2 * half], r1b, ydev)
    ca.wait()
    a1a[...] = a0[:, :, xq, :, 0:half] + r1a[...]
    da = exchange(3, a1a.at[:, 1 - yq], r2a, ydev)
    cb.wait()
    a1b[...] = a0[:, yq, :, :, half : 2 * half] + r1b[...]
    db = exchange(4, a1b.at[:, 1 - xq], r2b, xdev)
    da.wait()
    a2[:, :, 0:half] = a1a[:, yq] + r2a[...]
    db.wait()
    a2[:, :, half : 2 * half] = a1b[:, xq] + r2b[...]
    last_copies = [
        exchange(5 + d, a2.at[lax.rem(zq + d + 1, 4)], r3.at[d], zdevs[d]) for d in range(3)
    ]
    result = a2[zq]
    for d, copy in enumerate(last_copies):
        copy.wait()
        result = result + r3[d]
    low = lax.broadcasted_iota(jnp.int32, (16, LANE), 1) < 64
    reals, imags = [], []
    for j in range(2):
        even = result[:, 2 * j * LANE : (2 * j + 1) * LANE]
        odd = result[:, (2 * j + 1) * LANE : (2 * j + 2) * LANE]
        reals.append(jnp.where(low, even, pltpu.roll(odd, 64, 1)))
        imags.append(jnp.where(low, pltpu.roll(even, 64, 1), odd))
    out[...] = jnp.concatenate(reals + imags, axis=1)


def on_device(
    levels, conv_table, conv_bias, mix_weight, mix_bias, decoder, green_rows, green_cols, focal_order
):
    npx = lax.axis_size("px")
    npy = lax.axis_size("py")
    nrows, ncols = levels.shape
    wide = ncols + LANE
    scatter = npx == 16 and npy == 2
    width = CH * V
    height = U * Z
    rows = green_rows.transpose(2, 0, 1, 3).reshape(U, Z * 2 * nrows)
    cols = green_cols.reshape(Z * 2 * V, ncols)
    out_rows = 16 if scatter else height
    vmem = pl.BlockSpec(memory_space=pltpu.VMEM)
    half = width // 2
    rs = (lambda *shape: pltpu.VMEM(shape, F32)) if scatter else (lambda *shape: pltpu.VMEM((8, LANE), F32))
    result = pl.pallas_call(
        functools.partial(kernel, npx, npy, scatter),
        out_shape=jax.ShapeDtypeStruct((out_rows, width), F32),
        in_specs=[vmem] * 7 + [pl.BlockSpec(memory_space=pl.ANY), vmem],
        out_specs=vmem,
        scratch_shapes=[
            pltpu.VMEM((16, ncols), jnp.int32),
            pltpu.VMEM((32, LANE), jnp.int32),
            pltpu.VMEM((32, LANE), jnp.int32),
            pltpu.VMEM((3, 32, ncols), jnp.int32),
            pltpu.VMEM(((nrows + 2) * 3 * LEVELS, ncols), BF16),
            pltpu.VMEM((2 * HID, 192), F32),
            pltpu.VMEM((4 * HID, 4 * HID), F32),
            pltpu.VMEM((8 * KS * CH, 4 * HID), F32),
            pltpu.VMEM(((nrows + 2 * M) * KS * CH, ncols), F32),
            pltpu.VMEM(cols.shape, F32),
            pltpu.VMEM((cols.shape[0], LANE), F32),
            pltpu.VMEM((cols.shape[0], LANE), F32),
            pltpu.VMEM((cols.shape[0], wide), BF16),
            pltpu.VMEM(rows.shape, F32),
            pltpu.VMEM(rows.shape, F32),
            pltpu.VMEM((height, 512), BF16),
            pltpu.VMEM((512, width), BF16),
            rs(4, 2, 2, 32, width),
            rs(4, 2, 2, 16, width),
            rs(4, 2, 2, 16, width),
            rs(4, 2, 16, half),
            rs(4, 2, 16, half),
            rs(4, 2, 16, half),
            rs(4, 2, 16, half),
            rs(4, 16, half),
            rs(4, 16, half),
            rs(4, 16, width),
            rs(3, 16, width),
            pltpu.SemaphoreType.DMA((12,)),
            pltpu.SemaphoreType.DMA((12,)),
            pltpu.SemaphoreType.DMA((8,)),
            pltpu.SemaphoreType.DMA((8,)),
            pltpu.SemaphoreType.DMA,
        ],
        compiler_params=pltpu.CompilerParams(
            collective_id=0, has_side_effects=True, vmem_limit_bytes=48 * 1024 * 1024
        ),
    )(
        levels, conv_table, conv_bias.reshape(1, HID), mix_weight, mix_bias.reshape(1, HID),
        decoder, rows, cols, focal_order.reshape(1, U),
    )
    if scatter:
        return result.reshape(Z // npy, U // npx, width)
    own = lax.psum_scatter(result, ("px", "py"), scatter_dimension=0, tiled=True)
    own = own.reshape(Z // npy, U // npx, CH // 2, 2, V).transpose(0, 1, 3, 2, 4)
    return own.reshape(Z // npy, U // npx, width)


def solution(mesh):
    return jax.shard_map(
        on_device,
        mesh=mesh,
        in_specs=(
            P("px", "py"),
            P(),
            P(),
            P(),
            P(),
            P(),
            P(None, None, None, "px"),
            P(None, None, None, "py"),
            P(),
        ),
        out_specs=P("py", "px", None),
        check_vma=False,
    )
```

```python
import functools

import jax
import jax.numpy as jnp
from jax import lax
from jax.experimental import pallas as pl
from jax.experimental.pallas import tpu as pltpu
from jax.sharding import PartitionSpec as P

CH = 8
M = 2
KS = 5
Z = 8
U = 64
V = 64
LEVELS = 16
HID = 64
LANE = 128
MESH = pl.DeviceIdType.MESH
F32 = jnp.float32
BF16 = jnp.bfloat16


def gelu(half):
    inner = half * (1.5957691216057308 + (1.5957691216057308 * 4 * 0.044715) * (half * half))
    return half + half * jnp.tanh(inner)


def column(row):
    n = row.shape[1]
    here = lax.broadcasted_iota(jnp.int32, (n, n), 0) == lax.broadcasted_iota(jnp.int32, (n, n), 1)
    return jnp.sum(jnp.where(here, row, 0.0), axis=1, keepdims=True)


def nt_dot(a, b):
    return lax.dot_general(a, b, (((1,), (1,)), ((), ())), preferred_element_type=F32)


def kernel(
    npx, npy, scatter,
    lv_in, table_in, cb_in, mix_in, mb_in, dec_in, rows_in, cols_in, order_in, out,
    lv, table, conv_bias, mix, mix_bias, dec, rows, order,
    lvx, lv_right, lv_left, lvr, onehot, w1, w2, wd, taps, cols, cols_right, cols_left, colsb,
    rows_up, rows_down, lhs, rhs, field, r0, a0, r1a, r1b, a1a, a1b, r2a, r2b, a2, r3,
    send, recv, rs_send, rs_recv, load_sem,
):
    px = lax.axis_index("px")
    py = lax.axis_index("py")
    nrows, ncols = lv.shape
    wide = ncols + LANE
    ext = nrows + 2 * M

    up, down = lax.rem(px + npx - 1, npx), lax.rem(px + 1, npx)
    left, right = lax.rem(py + npy - 1, npy), lax.rem(py + 1, npy)
    greeted = [
        (up, py), (down, py), (px, left), (px, right),
        (up, left), (up, right), (down, left), (down, right),
    ]
    if scatter:
        xq = lax.rem(px, 2)
        yq = lax.rem(px // 2, 2)
        zq = px // 4
        xdev = (px + 1 - 2 * xq, py)
        ydev = (px + 2 - 4 * yq, py)
        zdevs = [(lax.rem(px + 4 * d, 16), py) for d in (1, 2, 3)]
        greeted += [xdev, ydev] + zdevs

    barrier = pltpu.get_barrier_semaphore()
    for device in greeted:
        pl.semaphore_signal(barrier, inc=1, device_id=device, device_id_type=MESH)
    loads = []
    for i, (src, dst) in enumerate([
        (table_in, table), (cb_in, conv_bias), (mix_in, mix), (mb_in, mix_bias), (dec_in, dec),
        (lv_in, lv), (rows_in, rows), (order_in, order), (cols_in, cols),
    ]):
        loads.append(pltpu.make_async_copy(src, dst, load_sem.at[i]))
        loads[-1].start()
    for load in loads[:5]:
        load.wait()

    w1[...] = jnp.zeros_like(w1)
    for r in range(2):
        w1[HID * r : HID * (r + 1), 48 * r : 48 * r + 144] = 0.5 * table[...].astype(F32)
    w2[...] = jnp.zeros_like(w2)
    for r in range(4):
        w2[HID * r : HID * (r + 1), HID * r : HID * (r + 1)] = 0.5 * mix[...].astype(F32)
    wd[...] = jnp.zeros_like(wd)
    for r in range(4):
        for t in range(KS):
            e = r + t
            wd[40 * e : 40 * (e + 1), HID * r : HID * (r + 1)] = dec[t].astype(F32)
    w1b = w1[...].astype(BF16)
    w2b = w2[...].astype(BF16)
    wdb = wd[...].astype(BF16)
    bias1 = column(0.5 * conv_bias[...])
    bias1 = jnp.concatenate([bias1, bias1], axis=0)
    bias2 = column(0.5 * mix_bias[...])
    bias2 = jnp.concatenate([bias2] * 4, axis=0)

    pl.semaphore_wait(barrier, len(greeted))

    def remote(slot, src, dst, device):
        copy = pltpu.make_async_remote_copy(
            src_ref=src, dst_ref=dst, send_sem=send.at[slot], recv_sem=recv.at[slot],
            device_id=device, device_id_type=MESH,
        )
        copy.start()
        return copy

    last = ncols - LANE
    side_copies = [
        remote(0, lv_in.at[:, 0:LANE], lv_right.at[8:24, :], (px, left)),
        remote(1, lv_in.at[:, last:ncols], lv_left.at[8:24, :], (px, right)),
    ]
    edge_copies = [
        remote(2, lv_in.at[nrows - 8 : nrows, :], lvx.at[0:8, :], (down, py)),
        remote(3, lv_in.at[0:8, :], lvx.at[8:16, :], (up, py)),
        remote(4, lv_in.at[nrows - 8 : nrows, 0:LANE], lv_right.at[0:8, :], (down, left)),
        remote(5, lv_in.at[nrows - 8 : nrows, last:ncols], lv_left.at[0:8, :], (down, right)),
        remote(6, lv_in.at[0:8, 0:LANE], lv_right.at[24:32, :], (up, left)),
        remote(7, lv_in.at[0:8, last:ncols], lv_left.at[24:32, :], (up, right)),
    ]
    green_copies = [
        remote(8, rows_in, rows_up, (down, py)),
        remote(9, rows_in, rows_down, (up, py)),
        remote(10, cols_in.at[:, 0:LANE], cols_right, (px, left)),
        remote(11, cols_in.at[:, last:ncols], cols_left, (px, right)),
    ]
    for load in loads[5:]:
        load.wait()
    colsb[:, 0:ncols] = cols[...].astype(BF16)

    first_up, last_down = px == 0, px == npx - 1
    first_left, last_right = py == 0, py == npy - 1
    ids = lax.broadcasted_iota(jnp.int32, (LEVELS, ncols), 0)

    def place(at, body, outside):
        n = body.shape[0]
        lane = lax.broadcasted_iota(jnp.int32, (n, LANE), 1)
        side = jnp.where(
            lane < 64,
            jnp.where(last_right, -1, lv_right[at : at + n, :]),
            jnp.where(first_left, -1, lv_left[at : at + n, :]),
        )
        whole = jnp.concatenate([body, side], axis=1)
        if outside is not None:
            whole = jnp.where(outside, -1, whole)
        lvr[0, at : at + n, :] = pltpu.roll(whole, 1, 1)[:, :ncols]
        lvr[1, at : at + n, :] = whole[:, :ncols]
        lvr[2, at : at + n, :] = pltpu.roll(whole, wide - 1, 1)[:, :ncols]

    def encode(i):
        for b in range(3):
            row = lvr[b, 7 + i : 8 + i, :]
            match = jnp.where(ids == row, 1.0, 0.0).astype(BF16)
            onehot[(3 * i + b) * LEVELS : (3 * i + b + 1) * LEVELS, :] = match

    def group(g):
        parts = []
        for r in range(2):
            first = 96 * (2 * g + r)
            act = jnp.dot(w1b, onehot[first : first + 192, :], preferred_element_type=F32) + bias1
            parts.append(gelu(act).astype(BF16))
        hidden = jnp.concatenate(parts, axis=0)
        act = jnp.dot(w2b, hidden, preferred_element_type=F32) + bias2
        features = gelu(act).astype(BF16)
        return jnp.dot(wdb, features, preferred_element_type=F32)

    for copy in side_copies:
        copy.wait()
    place(8, lv[...], None)
    for i in range(1, nrows + 1):
        encode(i)
    tap = group(1)
    taps[160:480, :] = tap
    tap = group(2)
    taps[320:480, :] += tap[0:160]
    taps[480:640, :] = tap[160:320]
    for copy in edge_copies:
        copy.wait()
    place(0, lvx[0:8, :], first_up)
    place(24, lvx[8:16, :], last_down)
    encode(0)
    encode(nrows + 1)
    tap = group(0)
    taps[0:160, :] = tap[0:160]
    taps[160:320, :] += tap[160:320]
    tap = group(3)
    taps[480:640, :] += tap[0:160]
    taps[640:800, :] = tap[160:320]

    for copy in green_copies:
        copy.wait()
    clane = lax.broadcasted_iota(jnp.int32, cols_right.shape, 1)
    colsb[:, ncols:wide] = jnp.where(
        clane < 64,
        jnp.where(last_right, 0.0, cols_right[...]),
        jnp.where(first_left, 0.0, cols_left[...]),
    ).astype(BF16)

    share = U // npx
    er = lax.broadcasted_iota(jnp.int32, (2 * U, U), 0)
    ec = lax.broadcasted_iota(jnp.int32, (2 * U, U), 1)
    pick = jnp.where((er // (2 * share)) * share + er % share == ec, 1.0, 0.0).astype(BF16)
    wr = lax.broadcasted_iota(jnp.int32, (U, U), 0)
    placed = jnp.where(wr == order[...], 1.0, 0.0).astype(BF16)
    pick = nt_dot(pick, placed).astype(BF16)
    xrow = lax.broadcasted_iota(jnp.int32, rows.shape, 0) % 16
    mixed = jnp.where(
        xrow < 8,
        jnp.where(last_down, 0.0, rows_down[...]),
        jnp.where(first_up, 0.0, rows_up[...]),
    ).astype(BF16)
    own = rows[...].astype(BF16)
    zr = (lax.broadcasted_iota(jnp.int32, (2 * U, LANE), 0) // share) % 2
    zc = (lax.broadcasted_iota(jnp.int32, (2 * U, LANE), 1) // 32) % 2
    for c in range(Z // 2):
        both = jnp.concatenate([own[64 * c : 64 * c + 64], mixed[64 * c : 64 * c + 64]], axis=0)
        lhs[c] = jnp.where(zr == zc, nt_dot(pick, both), 0.0).astype(BF16)

    blank = jnp.zeros((CH, LANE), F32)
    tiles = []
    for e in range(ext):
        total = None
        for s in range(KS):
            piece = jnp.concatenate([taps[40 * e + 8 * s : 40 * e + 8 * s + 8, :], blank], axis=1)
            if s != M:
                piece = pltpu.roll(piece, (s - M) % wide, 1)
            total = piece if total is None else total + piece
        tiles.append(total)
    near_field = jnp.concatenate(tiles, axis=0).astype(BF16)
    pr = lax.broadcasted_iota(jnp.int32, (CH * 32, CH * ext), 0)
    pc = lax.broadcasted_iota(jnp.int32, (CH * 32, CH * ext), 1)
    perm = jnp.where((pr // 32 == pc % 8) & ((pc // 8 + 30) % 32 == pr % 32), 1.0, 0.0).astype(BF16)
    near_field = jnp.dot(perm, near_field, preferred_element_type=F32).astype(BF16)
    sign = jnp.where(lax.broadcasted_iota(jnp.int32, (32, LANE), 1) < 64, -1.0, 1.0)

    def planes(c, slot):
        cut = pl.ds(pl.multiple_of(256 * c, 256), 256)
        sums = nt_dot(near_field, colsb[cut, :])
        for z in range(2):
            for p in range(CH // 2):
                one = sums[32 * p : 32 * p + 32, LANE * z : LANE * (z + 1)]
                two = sums[32 * p + 128 : 32 * p + 160, LANE * z : LANE * (z + 1)]
                at = slice(LANE * p, LANE * (p + 1))
                for k, value in enumerate((
                    one + sign * pltpu.roll(two, 64, 1), sign * pltpu.roll(one, 64, 1) - two
                )):
                    high = value.astype(BF16)
                    low = (value - high.astype(F32)).astype(BF16)
                    for source in range(2):
                        base = 64 * source + 32 * z + 16 * k
                        rhs[slot, 0, base : base + 16, at] = high[16 * source : 16 * source + 16]
                        rhs[slot, 1, base : base + 16, at] = low[16 * source : 16 * source + 16]
        left_side = lhs[c]
        return jnp.dot(left_side, rhs[slot, 0], preferred_element_type=F32) + jnp.dot(
            left_side, rhs[slot, 1], preferred_element_type=F32
        )

    if not scatter:
        for c in range(Z // 2):
            out[c] = planes(c, c)
        return

    def exchange(slot, src, dst, device):
        copy = pltpu.make_async_remote_copy(
            src_ref=src, dst_ref=dst, send_sem=rs_send.at[slot], recv_sem=rs_recv.at[slot],
            device_id=device, device_id_type=MESH,
        )
        copy.start()
        return copy

    half = a0.shape[-1] // 2
    core = []
    for i in range(2):
        field[i] = planes(2 * (1 - py) + i, i).reshape(field.shape[1:])
        core.append(exchange(i, field.at[i], r0.at[i], (px, 1 - py)))
    step1 = []
    for i in range(2):
        value = planes(2 * py + i, 2 + i).reshape(field.shape[1:])
        core[i].wait()
        a0[i] = value + r0[i]
        step1.append((
            exchange(2 + 7 * i, a0.at[i, :, :, 1 - xq, :, 0:half], r1a.at[i], xdev),
            exchange(3 + 7 * i, a0.at[i, :, 1 - yq, :, :, half : 2 * half], r1b.at[i], ydev),
        ))
    step2 = []
    for i in range(2):
        step1[i][0].wait()
        a1a[i] = a0[i, :, :, xq, :, 0:half] + r1a[i]
        da = exchange(4 + 7 * i, a1a.at[i, :, 1 - yq], r2a.at[i], ydev)
        step1[i][1].wait()
        a1b[i] = a0[i, :, yq, :, :, half : 2 * half] + r1b[i]
        db = exchange(5 + 7 * i, a1b.at[i, :, 1 - xq], r2b.at[i], xdev)
        step2.append((da, db))
    step3 = []
    for i in range(2):
        step2[i][0].wait()
        a2[i, :, :, 0:half] = a1a[i, :, yq] + r2a[i]
        step2[i][1].wait()
        a2[i, :, :, half : 2 * half] = a1b[i, :, xq] + r2b[i]
        step3.append([
            exchange(6 + 7 * i + d, a2.at[i, lax.rem(zq + d + 1, 4)], r3.at[i, d], zdevs[d])
            for d in range(3)
        ])
    low = lax.broadcasted_iota(jnp.int32, (8, LANE), 1) < 64
    for i in range(2):
        result = a2[i, zq]
        for d, copy in enumerate(step3[i]):
            copy.wait()
            result = result + r3[i, d]
        reals, imags = [], []
        for j in range(2):
            even = result[:, 2 * j * LANE : (2 * j + 1) * LANE]
            odd = result[:, (2 * j + 1) * LANE : (2 * j + 2) * LANE]
            reals.append(jnp.where(low, even, pltpu.roll(odd, 64, 1)))
            imags.append(jnp.where(low, pltpu.roll(even, 64, 1), odd))
        out[8 * i : 8 * i + 8, :] = jnp.concatenate(reals + imags, axis=1)


def on_device(
    levels, conv_table, conv_bias, mix_weight, mix_bias, decoder, green_rows, green_cols, focal_order
):
    npx = lax.axis_size("px")
    npy = lax.axis_size("py")
    nrows, ncols = levels.shape
    wide = ncols + LANE
    scatter = npx == 16 and npy == 2
    width = CH * V
    share = U // npx
    rows = green_rows.transpose(0, 1, 3, 2).reshape(Z * 2 * nrows, U)
    cols = green_cols.reshape(Z * 2 * V, ncols)
    operands = (
        levels, conv_table, conv_bias.reshape(1, HID), mix_weight, mix_bias.reshape(1, HID),
        decoder, rows, cols, focal_order.reshape(1, U),
    )
    half = width // 2

    def rs(*shape):
        return pltpu.VMEM(shape if scatter else (8, LANE), F32)

    def like(array):
        return pltpu.VMEM(array.shape, array.dtype)

    result = pl.pallas_call(
        functools.partial(kernel, npx, npy, scatter),
        out_shape=jax.ShapeDtypeStruct((16, width) if scatter else (Z // 2, 2 * U, width), F32),
        in_specs=[pl.BlockSpec(memory_space=pltpu.HBM)] * 9,
        out_specs=pl.BlockSpec(memory_space=pltpu.VMEM),
        scratch_shapes=[
            *[like(operands[i]) for i in (0, 1, 2, 3, 4, 5, 6, 8)],
            pltpu.VMEM((16, ncols), jnp.int32),
            pltpu.VMEM((32, LANE), jnp.int32),
            pltpu.VMEM((32, LANE), jnp.int32),
            pltpu.VMEM((3, 32, ncols), jnp.int32),
            pltpu.VMEM(((nrows + 2) * 3 * LEVELS, ncols), BF16),
            pltpu.VMEM((2 * HID, 192), F32),
            pltpu.VMEM((4 * HID, 4 * HID), F32),
            pltpu.VMEM((8 * KS * CH, 4 * HID), F32),
            pltpu.VMEM(((nrows + 2 * M) * KS * CH, ncols), F32),
            pltpu.VMEM(cols.shape, F32),
            pltpu.VMEM((cols.shape[0], LANE), F32),
            pltpu.VMEM((cols.shape[0], LANE), F32),
            pltpu.VMEM((cols.shape[0], wide), BF16),
            like(rows),
            like(rows),
            pltpu.VMEM((Z // 2, 2 * U, LANE), BF16),
            pltpu.VMEM((4, 2, LANE, width), BF16),
            rs(2, 4, 2, 2, 8, width),
            rs(2, 4, 2, 2, 8, width),
            rs(2, 4, 2, 2, 8, width),
            rs(2, 4, 2, 8, half),
            rs(2, 4, 2, 8, half),
            rs(2, 4, 2, 8, half),
            rs(2, 4, 2, 8, half),
            rs(2, 4, 8, half),
            rs(2, 4, 8, half),
            rs(2, 4, 8, width),
            rs(2, 3, 8, width),
            pltpu.SemaphoreType.DMA((12,)),
            pltpu.SemaphoreType.DMA((12,)),
            pltpu.SemaphoreType.DMA((16,)),
            pltpu.SemaphoreType.DMA((16,)),
            pltpu.SemaphoreType.DMA((9,)),
        ],
        compiler_params=pltpu.CompilerParams(
            collective_id=0, has_side_effects=True, vmem_limit_bytes=56 * 1024 * 1024
        ),
    )(*operands)
    if scatter:
        return result.reshape(Z // npy, share, width)
    result = result.reshape(Z // 2, npx, 2, share, width).transpose(1, 0, 2, 3, 4)
    own = lax.psum_scatter(result.reshape(Z * U, width), ("px", "py"), scatter_dimension=0, tiled=True)
    own = own.reshape(Z // npy, share, CH // 2, 2, V).transpose(0, 1, 3, 2, 4)
    return own.reshape(Z // npy, share, width)


def solution(mesh):
    return jax.shard_map(
        on_device,
        mesh=mesh,
        in_specs=(
            P("px", "py"),
            P(),
            P(),
            P(),
            P(),
            P(),
            P(None, None, None, "px"),
            P(None, None, None, "py"),
            P(),
        ),
        out_specs=P("py", "px", None),
        check_vma=False,
    )
```

```python
import functools

import jax
import jax.numpy as jnp
from jax import lax
from jax.experimental import pallas as pl
from jax.experimental.pallas import tpu as pltpu
from jax.sharding import PartitionSpec as P

CH = 8
M = 2
KS = 5
Z = 8
U = 64
V = 64
LEVELS = 16
HID = 64
LANE = 128
MESH = pl.DeviceIdType.MESH
F32 = jnp.float32
BF16 = jnp.bfloat16


def gelu(half):
    inner = half * (1.5957691216057308 + (1.5957691216057308 * 4 * 0.044715) * (half * half))
    return half + half * jnp.tanh(inner)


def column(row):
    n = row.shape[1]
    here = lax.broadcasted_iota(jnp.int32, (n, n), 0) == lax.broadcasted_iota(jnp.int32, (n, n), 1)
    return jnp.sum(jnp.where(here, row, 0.0), axis=1, keepdims=True)


def nt_dot(a, b):
    return lax.dot_general(a, b, (((1,), (1,)), ((), ())), preferred_element_type=F32)


def kernel(
    npx, npy, scatter,
    lv_in, table_in, cb_in, mix_in, mb_in, dec_in, rows_in, cols_in, order_in, out,
    lv, table, conv_bias, mix, mix_bias, dec, rows, order,
    lvx, lv_right, lv_left, lvr, onehot, w1, w2, wd, taps, cols, cols_right, cols_left, colsb,
    rows_up, rows_down, lhs, field, r0, a0, r1a, r1b, a1a, a1b, r2a, r2b, a2, r3,
    send, recv, rs_send, rs_recv, load_sem,
):
    px = lax.axis_index("px")
    py = lax.axis_index("py")
    nrows, ncols = lv.shape
    wide = ncols + LANE
    ext = nrows + 2 * M

    up, down = lax.rem(px + npx - 1, npx), lax.rem(px + 1, npx)
    left, right = lax.rem(py + npy - 1, npy), lax.rem(py + 1, npy)
    greeted = [
        (up, py), (down, py), (px, left), (px, right),
        (up, left), (up, right), (down, left), (down, right),
    ]
    if scatter:
        xq = lax.rem(px, 2)
        yq = lax.rem(px // 2, 2)
        zq = px // 4
        xdev = (px + 1 - 2 * xq, py)
        ydev = (px + 2 - 4 * yq, py)
        zdevs = [(lax.rem(px + 4 * d, 16), py) for d in (1, 2, 3)]
        greeted += [xdev, ydev] + zdevs

    barrier = pltpu.get_barrier_semaphore()
    for device in greeted:
        pl.semaphore_signal(barrier, inc=1, device_id=device, device_id_type=MESH)
    loads = []
    for i, (src, dst) in enumerate([
        (table_in, table), (cb_in, conv_bias), (mix_in, mix), (mb_in, mix_bias), (dec_in, dec),
        (lv_in, lv), (rows_in, rows), (order_in, order), (cols_in, cols),
    ]):
        loads.append(pltpu.make_async_copy(src, dst, load_sem.at[i]))
        loads[-1].start()
    for load in loads[:5]:
        load.wait()

    w1[...] = jnp.zeros_like(w1)
    for r in range(2):
        w1[HID * r : HID * (r + 1), 48 * r : 48 * r + 144] = 0.5 * table[...].astype(F32)
    w2[...] = jnp.zeros_like(w2)
    for r in range(4):
        w2[HID * r : HID * (r + 1), HID * r : HID * (r + 1)] = 0.5 * mix[...].astype(F32)
    wd[...] = jnp.zeros_like(wd)
    for r in range(4):
        for t in range(KS):
            e = r + t
            wd[40 * e : 40 * (e + 1), HID * r : HID * (r + 1)] = dec[t].astype(F32)
    w1b = w1[...].astype(BF16)
    w2b = w2[...].astype(BF16)
    wdb = wd[...].astype(BF16)
    bias1 = column(0.5 * conv_bias[...])
    bias1 = jnp.concatenate([bias1, bias1], axis=0)
    bias2 = column(0.5 * mix_bias[...])
    bias2 = jnp.concatenate([bias2] * 4, axis=0)

    pl.semaphore_wait(barrier, len(greeted))

    def remote(slot, src, dst, device):
        copy = pltpu.make_async_remote_copy(
            src_ref=src, dst_ref=dst, send_sem=send.at[slot], recv_sem=recv.at[slot],
            device_id=device, device_id_type=MESH,
        )
        copy.start()
        return copy

    last = ncols - LANE
    side_copies = [
        remote(0, lv_in.at[:, 0:LANE], lv_right.at[8:24, :], (px, left)),
        remote(1, lv_in.at[:, last:ncols], lv_left.at[8:24, :], (px, right)),
    ]
    edge_copies = [
        remote(2, lv_in.at[nrows - 8 : nrows, :], lvx.at[0:8, :], (down, py)),
        remote(3, lv_in.at[0:8, :], lvx.at[8:16, :], (up, py)),
        remote(4, lv_in.at[nrows - 8 : nrows, 0:LANE], lv_right.at[0:8, :], (down, left)),
        remote(5, lv_in.at[nrows - 8 : nrows, last:ncols], lv_left.at[0:8, :], (down, right)),
        remote(6, lv_in.at[0:8, 0:LANE], lv_right.at[24:32, :], (up, left)),
        remote(7, lv_in.at[0:8, last:ncols], lv_left.at[24:32, :], (up, right)),
    ]
    green_copies = [
        remote(8, rows_in, rows_up, (down, py)),
        remote(9, rows_in, rows_down, (up, py)),
        remote(10, cols_in.at[:, 0:LANE], cols_right, (px, left)),
        remote(11, cols_in.at[:, last:ncols], cols_left, (px, right)),
    ]
    for load in loads[5:]:
        load.wait()
    colsb[:, 0:ncols] = cols[...].astype(BF16)
    share = U // npx
    er = lax.broadcasted_iota(jnp.int32, (4 * U, U), 0)
    ec = lax.broadcasted_iota(jnp.int32, (4 * U, U), 1)
    pick = jnp.where((er // (4 * share)) * share + er % share == ec, 1.0, 0.0).astype(BF16)
    wr = lax.broadcasted_iota(jnp.int32, (U, U), 0)
    placed = jnp.where(wr == order[...], 1.0, 0.0).astype(BF16)
    pick = nt_dot(pick, placed).astype(BF16)

    first_up, last_down = px == 0, px == npx - 1
    first_left, last_right = py == 0, py == npy - 1
    ids = lax.broadcasted_iota(jnp.int32, (LEVELS, ncols), 0)

    def place(at, body, outside):
        n = body.shape[0]
        lane = lax.broadcasted_iota(jnp.int32, (n, LANE), 1)
        side = jnp.where(
            lane < 64,
            jnp.where(last_right, -1, lv_right[at : at + n, :]),
            jnp.where(first_left, -1, lv_left[at : at + n, :]),
        )
        whole = jnp.concatenate([body, side], axis=1)
        if outside is not None:
            whole = jnp.where(outside, -1, whole)
        lvr[0, at : at + n, :] = pltpu.roll(whole, 1, 1)[:, :ncols]
        lvr[1, at : at + n, :] = whole[:, :ncols]
        lvr[2, at : at + n, :] = pltpu.roll(whole, wide - 1, 1)[:, :ncols]

    def encode(i):
        for b in range(3):
            row = lvr[b, 7 + i : 8 + i, :]
            match = jnp.where(ids == row, 1.0, 0.0).astype(BF16)
            onehot[(3 * i + b) * LEVELS : (3 * i + b + 1) * LEVELS, :] = match

    def group(g):
        parts = []
        for r in range(2):
            first = 96 * (2 * g + r)
            act = jnp.dot(w1b, onehot[first : first + 192, :], preferred_element_type=F32) + bias1
            parts.append(gelu(act).astype(BF16))
        hidden = jnp.concatenate(parts, axis=0)
        act = jnp.dot(w2b, hidden, preferred_element_type=F32) + bias2
        features = gelu(act).astype(BF16)
        return jnp.dot(wdb, features, preferred_element_type=F32)

    for copy in side_copies:
        copy.wait()
    place(8, lv[...], None)
    for i in range(1, nrows + 1):
        encode(i)
    tap = group(1)
    taps[160:480, :] = tap
    tap = group(2)
    taps[320:480, :] += tap[0:160]
    taps[480:640, :] = tap[160:320]
    for copy in edge_copies:
        copy.wait()
    place(0, lvx[0:8, :], first_up)
    place(24, lvx[8:16, :], last_down)
    encode(0)
    encode(nrows + 1)
    tap = group(0)
    taps[0:160, :] = tap[0:160]
    taps[160:320, :] += tap[160:320]
    tap = group(3)
    taps[480:640, :] += tap[0:160]
    taps[640:800, :] = tap[160:320]

    for copy in green_copies:
        copy.wait()
    clane = lax.broadcasted_iota(jnp.int32, cols_right.shape, 1)
    colsb[:, ncols:wide] = jnp.where(
        clane < 64,
        jnp.where(last_right, 0.0, cols_right[...]),
        jnp.where(first_left, 0.0, cols_left[...]),
    ).astype(BF16)

    xrow = lax.broadcasted_iota(jnp.int32, rows.shape, 0) % 16
    mixed = jnp.where(
        xrow < 8,
        jnp.where(last_down, 0.0, rows_down[...]),
        jnp.where(first_up, 0.0, rows_up[...]),
    ).astype(BF16)
    own = rows[...].astype(BF16)
    pr = (lax.broadcasted_iota(jnp.int32, (4 * U, 2 * LANE), 0) // share) % 4
    pc = (lax.broadcasted_iota(jnp.int32, (4 * U, 2 * LANE), 1) // 32) % 4
    for z in range(Z):
        blocks = []
        for k in range(2):
            at = 32 * z + 16 * k
            blocks += [own[at : at + 16], mixed[at : at + 16]] * 4
        spread = nt_dot(pick, jnp.concatenate(blocks, axis=0))
        lhs[z] = jnp.where(pr == pc, spread, 0.0).astype(BF16)

    blank = jnp.zeros((CH, LANE), F32)
    tiles = []
    for e in range(ext):
        total = None
        for s in range(KS):
            piece = jnp.concatenate([taps[40 * e + 8 * s : 40 * e + 8 * s + 8, :], blank], axis=1)
            if s != M:
                piece = pltpu.roll(piece, (s - M) % wide, 1)
            total = piece if total is None else total + piece
        tiles.append(total)
    near_field = jnp.concatenate(tiles, axis=0).astype(BF16)
    pr = lax.broadcasted_iota(jnp.int32, (CH * 32, CH * ext), 0)
    pc = lax.broadcasted_iota(jnp.int32, (CH * 32, CH * ext), 1)
    perm = jnp.where((pr // 32 == pc % 8) & ((pc // 8 + 30) % 32 == pr % 32), 1.0, 0.0).astype(BF16)
    near_field = jnp.dot(perm, near_field, preferred_element_type=F32).astype(BF16)

    def planes(c):
        cut = pl.ds(pl.multiple_of(256 * c, 256), 256)
        sums = nt_dot(colsb[cut, :], near_field)
        fields = []
        for z in range(2):
            one = sums[LANE * z : LANE * z + LANE, 0:LANE]
            two = sums[LANE * z : LANE * z + LANE, LANE : 2 * LANE]
            real = one[0:64] - two[64:128]
            imag = one[64:128] + two[0:64]
            first = jnp.concatenate([real, imag], axis=0)
            second = jnp.concatenate([-imag, real], axis=0)
            value = jnp.concatenate([first, second], axis=1)
            high = value.astype(BF16)
            low = (value - high.astype(F32)).astype(BF16)
            left_side = lhs[2 * c + z]
            fields.append(nt_dot(left_side, high) + nt_dot(left_side, low))
        return fields

    if not scatter:
        for c in range(Z // 2):
            out[2 * c], out[2 * c + 1] = planes(c)
        return

    def exchange(slot, src, dst, device):
        copy = pltpu.make_async_remote_copy(
            src_ref=src, dst_ref=dst, send_sem=rs_send.at[slot], recv_sem=rs_recv.at[slot],
            device_id=device, device_id_type=MESH,
        )
        copy.start()
        return copy

    core = []
    for i in range(2):
        for z, value in enumerate(planes(2 * (1 - py) + i)):
            field[i, z] = value.reshape(field.shape[2:])
        core.append(exchange(i, field.at[i], r0.at[i], (px, 1 - py)))
    step1 = []
    for i in range(2):
        values = planes(2 * py + i)
        core[i].wait()
        for z in range(2):
            a0[i, z] = values[z].reshape(field.shape[2:]) + r0[i, z]
        step1.append((
            exchange(2 + 7 * i, a0.at[i, 0, :, :, 1 - xq], r1a.at[i], xdev),
            exchange(3 + 7 * i, a0.at[i, 1, :, 1 - yq], r1b.at[i], ydev),
        ))
    step2 = []
    for i in range(2):
        step1[i][0].wait()
        a1a[i] = a0[i, 0, :, :, xq] + r1a[i]
        da = exchange(4 + 7 * i, a1a.at[i, :, 1 - yq], r2a.at[i], ydev)
        step1[i][1].wait()
        a1b[i] = a0[i, 1, :, yq] + r1b[i]
        db = exchange(5 + 7 * i, a1b.at[i, :, 1 - xq], r2b.at[i], xdev)
        step2.append((da, db))
    step3 = []
    for i in range(2):
        step2[i][0].wait()
        a2[i, :, 0] = a1a[i, :, yq] + r2a[i]
        step2[i][1].wait()
        a2[i, :, 1] = a1b[i, :, xq] + r2b[i]
        step3.append([
            exchange(6 + 7 * i + d, a2.at[i, lax.rem(zq + d + 1, 4)], r3.at[i, d], zdevs[d])
            for d in range(3)
        ])
    first_half = lax.broadcasted_iota(jnp.int32, (share, LANE), 1) < 64
    for i in range(2):
        result = a2[i, zq]
        for d, copy in enumerate(step3[i]):
            copy.wait()
            result = result + r3[i, d]
        for z in range(2):
            reals, imags = [], []
            for j in range(2):
                even = result[z, 2 * j * share : (2 * j + 1) * share]
                odd = result[z, (2 * j + 1) * share : (2 * j + 2) * share]
                reals.append(jnp.where(first_half, even, pltpu.roll(odd, 64, 1)))
                imags.append(jnp.where(first_half, pltpu.roll(even, 64, 1), odd))
            out[2 * i + z] = jnp.concatenate(reals + imags, axis=1)


def on_device(
    levels, conv_table, conv_bias, mix_weight, mix_bias, decoder, green_rows, green_cols, focal_order
):
    npx = lax.axis_size("px")
    npy = lax.axis_size("py")
    nrows, ncols = levels.shape
    wide = ncols + LANE
    scatter = npx == 16 and npy == 2
    width = CH * V
    share = U // npx
    rows = green_rows.transpose(0, 1, 3, 2).reshape(Z * 2 * nrows, U)
    cols = green_cols.reshape(Z * 2 * V, ncols)
    operands = (
        levels, conv_table, conv_bias.reshape(1, HID), mix_weight, mix_bias.reshape(1, HID),
        decoder, rows, cols, focal_order.reshape(1, U),
    )

    def rs(*shape):
        return pltpu.VMEM(shape if scatter else (8, LANE), F32)

    def like(array):
        return pltpu.VMEM(array.shape, array.dtype)

    result = pl.pallas_call(
        functools.partial(kernel, npx, npy, scatter),
        out_shape=jax.ShapeDtypeStruct((Z // npy, share, width) if scatter else (Z, 4 * U, 2 * V), F32),
        in_specs=[pl.BlockSpec(memory_space=pltpu.HBM)] * 9,
        out_specs=pl.BlockSpec(memory_space=pltpu.VMEM),
        scratch_shapes=[
            *[like(operands[i]) for i in (0, 1, 2, 3, 4, 5, 6, 8)],
            pltpu.VMEM((16, ncols), jnp.int32),
            pltpu.VMEM((32, LANE), jnp.int32),
            pltpu.VMEM((32, LANE), jnp.int32),
            pltpu.VMEM((3, 32, ncols), jnp.int32),
            pltpu.VMEM(((nrows + 2) * 3 * LEVELS, ncols), BF16),
            pltpu.VMEM((2 * HID, 192), F32),
            pltpu.VMEM((4 * HID, 4 * HID), F32),
            pltpu.VMEM((8 * KS * CH, 4 * HID), F32),
            pltpu.VMEM(((nrows + 2 * M) * KS * CH, ncols), F32),
            pltpu.VMEM(cols.shape, F32),
            pltpu.VMEM((cols.shape[0], LANE), F32),
            pltpu.VMEM((cols.shape[0], LANE), F32),
            pltpu.VMEM((cols.shape[0], wide), BF16),
            like(rows),
            like(rows),
            pltpu.VMEM((Z, 4 * U, 2 * LANE), BF16),
            rs(2, 2, 4, 2, 2, 16, LANE),
            rs(2, 2, 4, 2, 2, 16, LANE),
            rs(2, 2, 4, 2, 2, 16, LANE),
            rs(2, 4, 2, 16, LANE),
            rs(2, 4, 2, 16, LANE),
            rs(2, 4, 2, 16, LANE),
            rs(2, 4, 2, 16, LANE),
            rs(2, 4, 16, LANE),
            rs(2, 4, 16, LANE),
            rs(2, 4, 2, 16, LANE),
            rs(2, 3, 2, 16, LANE),
            pltpu.SemaphoreType.DMA((12,)),
            pltpu.SemaphoreType.DMA((12,)),
            pltpu.SemaphoreType.DMA((16,)),
            pltpu.SemaphoreType.DMA((16,)),
            pltpu.SemaphoreType.DMA((9,)),
        ],
        compiler_params=pltpu.CompilerParams(
            collective_id=0, has_side_effects=True, vmem_limit_bytes=56 * 1024 * 1024
        ),
    )(*operands)
    if scatter:
        return result
    result = result.reshape(Z, npx, 4 * share, 2 * V).transpose(1, 0, 2, 3)
    own = lax.psum_scatter(
        result.reshape(npx * Z, 4 * share * 2 * V), ("px", "py"), scatter_dimension=0, tiled=True
    )
    own = own.reshape(Z // npy, CH // 2, share, 2, V).transpose(0, 2, 3, 1, 4)
    return own.reshape(Z // npy, share, width)


def solution(mesh):
    return jax.shard_map(
        on_device,
        mesh=mesh,
        in_specs=(
            P("px", "py"),
            P(),
            P(),
            P(),
            P(),
            P(),
            P(None, None, None, "px"),
            P(None, None, None, "py"),
            P(),
        ),
        out_specs=P("py", "px", None),
        check_vma=False,
    )
```

```python
import functools

import jax
import jax.numpy as jnp
from jax import lax
from jax.experimental import pallas as pl
from jax.experimental.pallas import tpu as pltpu
from jax.sharding import PartitionSpec as P

CH = 8
M = 2
KS = 5
Z = 8
U = 64
V = 64
LEVELS = 16
HID = 64
LANE = 128
MESH = pl.DeviceIdType.MESH
F32 = jnp.float32
BF16 = jnp.bfloat16


def gelu(half):
    inner = half * (1.5957691216057308 + (1.5957691216057308 * 4 * 0.044715) * (half * half))
    return half + half * jnp.tanh(inner)


def column(row):
    n = row.shape[1]
    here = lax.broadcasted_iota(jnp.int32, (n, n), 0) == lax.broadcasted_iota(jnp.int32, (n, n), 1)
    return jnp.sum(jnp.where(here, row, 0.0), axis=1, keepdims=True)


def nt_dot(a, b):
    return lax.dot_general(a, b, (((1,), (1,)), ((), ())), preferred_element_type=F32)


def kernel(
    npx, npy, scatter,
    lv_in, table_in, cb_in, mix_in, mb_in, dec_in, rows_in, cols_in, order_in, out,
    lv, table, conv_bias, mix, mix_bias, dec, rows, order,
    lvx, lv_right, lv_left, lvr, onehot, w1, w2, wd, biases, taps, cols, cols_right, cols_left, colsb,
    rows_up, rows_down, lhs, field, r0, a0, r1a, r1b, a1a, a1b, r2a, r2b, a2, r3,
    send, recv, rs_send, rs_recv, load_sem,
):
    px = lax.axis_index("px")
    py = lax.axis_index("py")
    nrows, ncols = lv.shape
    wide = ncols + LANE
    ext = nrows + 2 * M

    up, down = lax.rem(px + npx - 1, npx), lax.rem(px + 1, npx)
    left, right = lax.rem(py + npy - 1, npy), lax.rem(py + 1, npy)
    greeted = [
        (up, py), (down, py), (px, left), (px, right),
        (up, left), (up, right), (down, left), (down, right),
    ]
    if scatter:
        xq = lax.rem(px, 2)
        yq = lax.rem(px // 2, 2)
        zq = px // 4
        xdev = (px + 1 - 2 * xq, py)
        ydev = (px + 2 - 4 * yq, py)
        zdevs = [(lax.rem(px + 4 * d, 16), py) for d in (1, 2, 3)]
        greeted += [xdev, ydev] + zdevs

    barrier = pltpu.get_barrier_semaphore()
    for device in greeted:
        pl.semaphore_signal(barrier, inc=1, device_id=device, device_id_type=MESH)
    loads = []
    for i, (src, dst) in enumerate([
        (table_in, table), (cb_in, conv_bias), (mix_in, mix), (mb_in, mix_bias), (dec_in, dec),
        (lv_in, lv), (rows_in, rows), (order_in, order), (cols_in, cols),
    ]):
        loads.append(pltpu.make_async_copy(src, dst, load_sem.at[i]))
        loads[-1].start()
    pl.semaphore_wait(barrier, len(greeted))

    def remote(slot, src, dst, device):
        copy = pltpu.make_async_remote_copy(
            src_ref=src, dst_ref=dst, send_sem=send.at[slot], recv_sem=recv.at[slot],
            device_id=device, device_id_type=MESH,
        )
        copy.start()
        return copy

    last = ncols - LANE
    side_copies = [
        remote(0, lv_in.at[:, 0:LANE], lv_right.at[8:24, :], (px, left)),
        remote(1, lv_in.at[:, last:ncols], lv_left.at[8:24, :], (px, right)),
    ]
    edge_copies = [
        remote(2, lv_in.at[nrows - 8 : nrows, :], lvx.at[0:8, :], (down, py)),
        remote(3, lv_in.at[0:8, :], lvx.at[8:16, :], (up, py)),
        remote(4, lv_in.at[nrows - 8 : nrows, 0:LANE], lv_right.at[0:8, :], (down, left)),
        remote(5, lv_in.at[nrows - 8 : nrows, last:ncols], lv_left.at[0:8, :], (down, right)),
        remote(6, lv_in.at[0:8, 0:LANE], lv_right.at[24:32, :], (up, left)),
        remote(7, lv_in.at[0:8, last:ncols], lv_left.at[24:32, :], (up, right)),
    ]
    green_copies = [
        remote(8, rows_in, rows_up, (down, py)),
        remote(9, rows_in, rows_down, (up, py)),
        remote(10, cols_in.at[:, 0:LANE], cols_right, (px, left)),
        remote(11, cols_in.at[:, last:ncols], cols_left, (px, right)),
    ]
    for load in loads[:5]:
        load.wait()

    w1[...] = jnp.zeros_like(w1)
    for r in range(2):
        w1[HID * r : HID * (r + 1), 48 * r : 48 * r + 144] = 0.5 * table[...].astype(F32)
    w2[...] = jnp.zeros_like(w2)
    for r in range(4):
        w2[HID * r : HID * (r + 1), HID * r : HID * (r + 1)] = 0.5 * mix[...].astype(F32)
    wd[...] = jnp.zeros_like(wd)
    for r in range(4):
        for t in range(KS):
            e = r + t
            wd[40 * e : 40 * (e + 1), HID * r : HID * (r + 1)] = dec[t].astype(F32)
    w1b = w1[...].astype(BF16)
    w2b = w2[...].astype(BF16)
    wdb = wd[...].astype(BF16)
    bias1 = jnp.broadcast_to(column(0.5 * conv_bias[...]), (HID, LANE))
    bias2 = jnp.broadcast_to(column(0.5 * mix_bias[...]), (HID, LANE))
    for r in range(2):
        biases[HID * r : HID * (r + 1)] = bias1
    for r in range(2, 6):
        biases[HID * r : HID * (r + 1)] = bias2

    first_up, last_down = px == 0, px == npx - 1
    first_left, last_right = py == 0, py == npy - 1
    tile = 256
    count = ncols // tile
    inner, outer = range(1, count - 1), (0, count - 1)
    ids = lax.broadcasted_iota(jnp.int32, (LEVELS, tile), 0)

    def place(at, body, outside):
        n = body.shape[0]
        lane = lax.broadcasted_iota(jnp.int32, (n, LANE), 1)
        side = jnp.where(
            lane < 64,
            jnp.where(last_right, -1, lv_right[at : at + n, :]),
            jnp.where(first_left, -1, lv_left[at : at + n, :]),
        )
        whole = jnp.concatenate([body, side], axis=1)
        if outside is not None:
            whole = jnp.where(outside, -1, whole)
        lvr[0, at : at + n, :] = pltpu.roll(whole, 1, 1)[:, :ncols]
        lvr[1, at : at + n, :] = whole[:, :ncols]
        lvr[2, at : at + n, :] = pltpu.roll(whole, wide - 1, 1)[:, :ncols]

    def encode(i, t):
        at = slice(tile * t, tile * (t + 1))
        for b in range(3):
            row = lvr[b, 7 + i : 8 + i, at]
            match = jnp.where(ids == row, 1.0, 0.0).astype(BF16)
            onehot[(3 * i + b) * LEVELS : (3 * i + b + 1) * LEVELS, at] = match

    def first_layer(g, t):
        at = slice(tile * t, tile * (t + 1))
        bias = jnp.concatenate([biases[0 : 2 * HID]] * 2, axis=1)
        parts = []
        for r in range(2):
            first = 96 * (2 * g + r)
            act = jnp.dot(w1b, onehot[first : first + 192, at], preferred_element_type=F32) + bias
            parts.append(gelu(act).astype(BF16))
        return jnp.concatenate(parts, axis=0)

    def second_layer(hidden):
        bias = jnp.concatenate([biases[2 * HID : 6 * HID]] * 2, axis=1)
        act = jnp.dot(w2b, hidden, preferred_element_type=F32) + bias
        return gelu(act).astype(BF16)

    def decode(g, t, features):
        at = slice(tile * t, tile * (t + 1))
        tap = jnp.dot(wdb, features, preferred_element_type=F32)
        for part in range(2):
            first = 160 * (g + part)
            value = tap[160 * part : 160 * (part + 1)]
            if (g, part) in ((1, 0), (1, 1), (2, 1), (0, 0), (3, 1)):
                taps[first : first + 160, at] = value
            else:
                taps[first : first + 160, at] += value

    def network(blocks):
        hidden, features = {}, {}
        for step in range(len(blocks) + 2):
            if step < len(blocks):
                hidden[step] = first_layer(*blocks[step])
            if 1 <= step <= len(blocks):
                features[step - 1] = second_layer(hidden.pop(step - 1))
            if step >= 2:
                decode(*blocks[step - 2], features.pop(step - 2))

    loads[5].wait()
    lvr[0, 8:24, :] = pltpu.roll(lv[...], 1, 1)
    lvr[1, 8:24, :] = lv[...]
    lvr[2, 8:24, :] = pltpu.roll(lv[...], ncols - 1, 1)
    for i in range(1, nrows + 1):
        for t in inner:
            encode(i, t)
    network([(g, t) for g in (1, 2) for t in inner])
    for load in loads[6:]:
        load.wait()
    colsb[:, 0:ncols] = cols[...].astype(BF16)
    share = U // npx
    er = lax.broadcasted_iota(jnp.int32, (4 * U, U), 0)
    ec = lax.broadcasted_iota(jnp.int32, (4 * U, U), 1)
    pick = jnp.where((er // (4 * share)) * share + er % share == ec, 1.0, 0.0).astype(BF16)
    wr = lax.broadcasted_iota(jnp.int32, (U, U), 0)
    placed = jnp.where(wr == order[...], 1.0, 0.0).astype(BF16)
    pick = nt_dot(pick, placed).astype(BF16)

    for copy in side_copies:
        copy.wait()
    place(8, lv[...], None)
    for i in range(1, nrows + 1):
        for t in outer:
            encode(i, t)
    network([(g, t) for g in (1, 2) for t in outer])
    for copy in green_copies:
        copy.wait()
    clane = lax.broadcasted_iota(jnp.int32, cols_right.shape, 1)
    colsb[:, ncols:wide] = jnp.where(
        clane < 64,
        jnp.where(last_right, 0.0, cols_right[...]),
        jnp.where(first_left, 0.0, cols_left[...]),
    ).astype(BF16)

    xrow = lax.broadcasted_iota(jnp.int32, rows.shape, 0) % 16
    mixed = jnp.where(
        xrow < 8,
        jnp.where(last_down, 0.0, rows_down[...]),
        jnp.where(first_up, 0.0, rows_up[...]),
    ).astype(BF16)
    own = rows[...].astype(BF16)
    pr = (lax.broadcasted_iota(jnp.int32, (4 * U, 2 * LANE), 0) // share) % 4
    pc = (lax.broadcasted_iota(jnp.int32, (4 * U, 2 * LANE), 1) // 32) % 4
    for z in range(Z):
        blocks = []
        for k in range(2):
            at = 32 * z + 16 * k
            blocks += [own[at : at + 16], mixed[at : at + 16]] * 4
        spread = nt_dot(pick, jnp.concatenate(blocks, axis=0))
        lhs[z] = jnp.where(pr == pc, spread, 0.0).astype(BF16)

    for copy in edge_copies:
        copy.wait()
    place(0, lvx[0:8, :], first_up)
    place(24, lvx[8:16, :], last_down)
    for i in (0, nrows + 1):
        for t in range(count):
            encode(i, t)
    network([(g, t) for g in (0, 3) for t in range(count)])

    blank = jnp.zeros((CH, LANE), F32)
    tiles = []
    for e in range(ext):
        total = None
        for s in range(KS):
            piece = jnp.concatenate([taps[40 * e + 8 * s : 40 * e + 8 * s + 8, :], blank], axis=1)
            if s != M:
                piece = pltpu.roll(piece, (s - M) % wide, 1)
            total = piece if total is None else total + piece
        tiles.append(total)
    near_field = jnp.concatenate(tiles, axis=0).astype(BF16)
    pr = lax.broadcasted_iota(jnp.int32, (CH * 32, CH * ext), 0)
    pc = lax.broadcasted_iota(jnp.int32, (CH * 32, CH * ext), 1)
    perm = jnp.where((pr // 32 == pc % 8) & ((pc // 8 + 30) % 32 == pr % 32), 1.0, 0.0).astype(BF16)
    near_field = jnp.dot(perm, near_field, preferred_element_type=F32).astype(BF16)

    def planes(c):
        cut = pl.ds(pl.multiple_of(256 * c, 256), 256)
        sums = nt_dot(colsb[cut, :], near_field)
        fields = []
        for z in range(2):
            one = sums[LANE * z : LANE * z + LANE, 0:LANE]
            two = sums[LANE * z : LANE * z + LANE, LANE : 2 * LANE]
            real = one[0:64] - two[64:128]
            imag = one[64:128] + two[0:64]
            first = jnp.concatenate([real, imag], axis=0)
            second = jnp.concatenate([-imag, real], axis=0)
            value = jnp.concatenate([first, second], axis=1)
            high = value.astype(BF16)
            low = (value - high.astype(F32)).astype(BF16)
            left_side = lhs[2 * c + z]
            fields.append(nt_dot(left_side, high) + nt_dot(left_side, low))
        return fields

    if not scatter:
        for c in range(Z // 2):
            out[2 * c], out[2 * c + 1] = planes(c)
        return

    def exchange(slot, src, dst, device):
        copy = pltpu.make_async_remote_copy(
            src_ref=src, dst_ref=dst, send_sem=rs_send.at[slot], recv_sem=rs_recv.at[slot],
            device_id=device, device_id_type=MESH,
        )
        copy.start()
        return copy

    core = []
    for i in range(2):
        for z, value in enumerate(planes(2 * (1 - py) + i)):
            field[i, z] = value.reshape(field.shape[2:])
        core.append(exchange(i, field.at[i], r0.at[i], (px, 1 - py)))
    step1 = []
    for i in range(2):
        values = planes(2 * py + i)
        core[i].wait()
        for z in range(2):
            a0[i, z] = values[z].reshape(field.shape[2:]) + r0[i, z]
        step1.append((
            exchange(2 + 7 * i, a0.at[i, 0, :, :, 1 - xq], r1a.at[i], xdev),
            exchange(3 + 7 * i, a0.at[i, 1, :, 1 - yq], r1b.at[i], ydev),
        ))
    step2 = []
    for i in range(2):
        step1[i][0].wait()
        a1a[i] = a0[i, 0, :, :, xq] + r1a[i]
        da = exchange(4 + 7 * i, a1a.at[i, :, 1 - yq], r2a.at[i], ydev)
        step1[i][1].wait()
        a1b[i] = a0[i, 1, :, yq] + r1b[i]
        db = exchange(5 + 7 * i, a1b.at[i, :, 1 - xq], r2b.at[i], xdev)
        step2.append((da, db))
    step3 = []
    for i in range(2):
        step2[i][0].wait()
        a2[i, :, 0] = a1a[i, :, yq] + r2a[i]
        step2[i][1].wait()
        a2[i, :, 1] = a1b[i, :, xq] + r2b[i]
        step3.append([
            exchange(6 + 7 * i + d, a2.at[i, lax.rem(zq + d + 1, 4)], r3.at[i, d], zdevs[d])
            for d in range(3)
        ])
    first_half = lax.broadcasted_iota(jnp.int32, (share, LANE), 1) < 64
    for i in range(2):
        result = a2[i, zq]
        for d, copy in enumerate(step3[i]):
            copy.wait()
            result = result + r3[i, d]
        for z in range(2):
            reals, imags = [], []
            for j in range(2):
                even = result[z, 2 * j * share : (2 * j + 1) * share]
                odd = result[z, (2 * j + 1) * share : (2 * j + 2) * share]
                reals.append(jnp.where(first_half, even, pltpu.roll(odd, 64, 1)))
                imags.append(jnp.where(first_half, pltpu.roll(even, 64, 1), odd))
            out[2 * i + z] = jnp.concatenate(reals + imags, axis=1)


def on_device(
    levels, conv_table, conv_bias, mix_weight, mix_bias, decoder, green_rows, green_cols, focal_order
):
    npx = lax.axis_size("px")
    npy = lax.axis_size("py")
    nrows, ncols = levels.shape
    wide = ncols + LANE
    scatter = npx == 16 and npy == 2
    width = CH * V
    share = U // npx
    rows = green_rows.transpose(0, 1, 3, 2).reshape(Z * 2 * nrows, U)
    cols = green_cols.reshape(Z * 2 * V, ncols)
    operands = (
        levels, conv_table, conv_bias.reshape(1, HID), mix_weight, mix_bias.reshape(1, HID),
        decoder, rows, cols, focal_order.reshape(1, U),
    )

    def rs(*shape):
        return pltpu.VMEM(shape if scatter else (8, LANE), F32)

    def like(array):
        return pltpu.VMEM(array.shape, array.dtype)

    result = pl.pallas_call(
        functools.partial(kernel, npx, npy, scatter),
        out_shape=jax.ShapeDtypeStruct((Z // npy, share, width) if scatter else (Z, 4 * U, 2 * V), F32),
        in_specs=[pl.BlockSpec(memory_space=pltpu.HBM)] * 9,
        out_specs=pl.BlockSpec(memory_space=pltpu.VMEM),
        scratch_shapes=[
            *[like(operands[i]) for i in (0, 1, 2, 3, 4, 5, 6, 8)],
            pltpu.VMEM((16, ncols), jnp.int32),
            pltpu.VMEM((32, LANE), jnp.int32),
            pltpu.VMEM((32, LANE), jnp.int32),
            pltpu.VMEM((3, 32, ncols), jnp.int32),
            pltpu.VMEM(((nrows + 2) * 3 * LEVELS, ncols), BF16),
            pltpu.VMEM((2 * HID, 192), F32),
            pltpu.VMEM((4 * HID, 4 * HID), F32),
            pltpu.VMEM((8 * KS * CH, 4 * HID), F32),
            pltpu.VMEM((6 * HID, LANE), F32),
            pltpu.VMEM(((nrows + 2 * M) * KS * CH, ncols), F32),
            pltpu.VMEM(cols.shape, F32),
            pltpu.VMEM((cols.shape[0], LANE), F32),
            pltpu.VMEM((cols.shape[0], LANE), F32),
            pltpu.VMEM((cols.shape[0], wide), BF16),
            like(rows),
            like(rows),
            pltpu.VMEM((Z, 4 * U, 2 * LANE), BF16),
            rs(2, 2, 4, 2, 2, 16, LANE),
            rs(2, 2, 4, 2, 2, 16, LANE),
            rs(2, 2, 4, 2, 2, 16, LANE),
            rs(2, 4, 2, 16, LANE),
            rs(2, 4, 2, 16, LANE),
            rs(2, 4, 2, 16, LANE),
            rs(2, 4, 2, 16, LANE),
            rs(2, 4, 16, LANE),
            rs(2, 4, 16, LANE),
            rs(2, 4, 2, 16, LANE),
            rs(2, 3, 2, 16, LANE),
            pltpu.SemaphoreType.DMA((12,)),
            pltpu.SemaphoreType.DMA((12,)),
            pltpu.SemaphoreType.DMA((16,)),
            pltpu.SemaphoreType.DMA((16,)),
            pltpu.SemaphoreType.DMA((9,)),
        ],
        compiler_params=pltpu.CompilerParams(
            collective_id=0, has_side_effects=True, vmem_limit_bytes=56 * 1024 * 1024
        ),
    )(*operands)
    if scatter:
        return result
    result = result.reshape(Z, npx, 4 * share, 2 * V).transpose(1, 0, 2, 3)
    own = lax.psum_scatter(
        result.reshape(npx * Z, 4 * share * 2 * V), ("px", "py"), scatter_dimension=0, tiled=True
    )
    own = own.reshape(Z // npy, CH // 2, share, 2, V).transpose(0, 2, 3, 1, 4)
    return own.reshape(Z // npy, share, width)


def solution(mesh):
    return jax.shard_map(
        on_device,
        mesh=mesh,
        in_specs=(
            P("px", "py"),
            P(),
            P(),
            P(),
            P(),
            P(),
            P(None, None, None, "px"),
            P(None, None, None, "py"),
            P(),
        ),
        out_specs=P("py", "px", None),
        check_vma=False,
    )
```

```python
import functools

import jax
import jax.numpy as jnp
from jax import lax
from jax.experimental import pallas as pl
from jax.experimental.pallas import tpu as pltpu
from jax.sharding import PartitionSpec as P

CH = 8
M = 2
KS = 5
Z = 8
U = 64
V = 64
LEVELS = 16
HID = 64
LANE = 128
MESH = pl.DeviceIdType.MESH
F32 = jnp.float32
BF16 = jnp.bfloat16


def gelu(half):
    inner = half * (1.5957691216057308 + (1.5957691216057308 * 4 * 0.044715) * (half * half))
    return half + half * jnp.tanh(inner)


def column(row):
    n = row.shape[1]
    here = lax.broadcasted_iota(jnp.int32, (n, n), 0) == lax.broadcasted_iota(jnp.int32, (n, n), 1)
    return jnp.sum(jnp.where(here, row, 0.0), axis=1, keepdims=True)


def nt_dot(a, b):
    return lax.dot_general(a, b, (((1,), (1,)), ((), ())), preferred_element_type=F32)


def kernel(
    npx, npy, scatter,
    lv_in, table_in, cb_in, mix_in, mb_in, dec_in, rows_in, cols_in, order_in, out,
    lv, table, conv_bias, mix, mix_bias, dec, rows, order,
    lvx, lv_right, lv_left, lvr, onehot, w1, w2, wd, taps, cols, cols_right, cols_left, colsb,
    rows_up, rows_down, rows_edge, cols_edge, lhs, field, r0, a0, r1a, r1b, a1a, a1b, r2a, r2b, a2, r3,
    send, recv, rs_send, rs_recv, load_sem,
):
    px = lax.axis_index("px")
    py = lax.axis_index("py")
    nrows, ncols = lv.shape
    wide = ncols + LANE
    ext = nrows + 2 * M

    up, down = lax.rem(px + npx - 1, npx), lax.rem(px + 1, npx)
    left, right = lax.rem(py + npy - 1, npy), lax.rem(py + 1, npy)
    greeted = [
        (up, py), (down, py), (px, left), (px, right),
        (up, left), (up, right), (down, left), (down, right),
    ]
    if scatter:
        xq = lax.rem(px, 2)
        yq = lax.rem(px // 2, 2)
        zq = px // 4
        xdev = (px + 1 - 2 * xq, py)
        ydev = (px + 2 - 4 * yq, py)
        zdevs = [(lax.rem(px + 4 * d, 16), py) for d in (1, 2, 3)]
        greeted += [xdev, ydev] + zdevs

    barrier = pltpu.get_barrier_semaphore()
    for device in greeted:
        pl.semaphore_signal(barrier, inc=1, device_id=device, device_id_type=MESH)
    loads = []
    for i, (src, dst) in enumerate([
        (table_in, table), (cb_in, conv_bias), (mix_in, mix), (mb_in, mix_bias), (dec_in, dec),
        (lv_in, lv), (rows_in, rows), (order_in, order), (cols_in, cols),
    ]):
        loads.append(pltpu.make_async_copy(src, dst, load_sem.at[i]))
        loads[-1].start()
    for load in loads[:5]:
        load.wait()

    w1[...] = jnp.zeros_like(w1)
    for r in range(2):
        w1[HID * r : HID * (r + 1), 48 * r : 48 * r + 144] = 0.5 * table[...].astype(F32)
    w2[...] = jnp.zeros_like(w2)
    for r in range(4):
        w2[HID * r : HID * (r + 1), HID * r : HID * (r + 1)] = 0.5 * mix[...].astype(F32)
    wd[...] = jnp.zeros_like(wd)
    for r in range(4):
        for t in range(KS):
            e = r + t
            wd[40 * e : 40 * (e + 1), HID * r : HID * (r + 1)] = dec[t].astype(F32)
    w1b = w1[...].astype(BF16)
    w2b = w2[...].astype(BF16)
    wdb = wd[...].astype(BF16)
    bias1 = column(0.5 * conv_bias[...])
    bias1 = jnp.concatenate([bias1, bias1], axis=0)
    bias2 = column(0.5 * mix_bias[...])
    bias2 = jnp.concatenate([bias2] * 4, axis=0)

    pl.semaphore_wait(barrier, len(greeted))

    def remote(slot, src, dst, device):
        copy = pltpu.make_async_remote_copy(
            src_ref=src, dst_ref=dst, send_sem=send.at[slot], recv_sem=recv.at[slot],
            device_id=device, device_id_type=MESH,
        )
        copy.start()
        return copy

    last = ncols - LANE
    side_copies = [
        remote(0, lv_in.at[:, 0:LANE], lv_right.at[8:24, :], (px, left)),
        remote(1, lv_in.at[:, last:ncols], lv_left.at[8:24, :], (px, right)),
    ]
    edge_copies = [
        remote(2, lv_in.at[nrows - 8 : nrows, :], lvx.at[0:8, :], (down, py)),
        remote(3, lv_in.at[0:8, :], lvx.at[8:16, :], (up, py)),
        remote(4, lv_in.at[nrows - 8 : nrows, 0:LANE], lv_right.at[0:8, :], (down, left)),
        remote(5, lv_in.at[nrows - 8 : nrows, last:ncols], lv_left.at[0:8, :], (down, right)),
        remote(6, lv_in.at[0:8, 0:LANE], lv_right.at[24:32, :], (up, left)),
        remote(7, lv_in.at[0:8, last:ncols], lv_left.at[24:32, :], (up, right)),
    ]
    for load in loads[5:]:
        load.wait()
    colsb[:, 0:ncols] = cols[...].astype(BF16)

    def grid(shape):
        return lax.broadcasted_iota(jnp.int32, shape, 0), lax.broadcasted_iota(jnp.int32, shape, 1)

    def mark(where):
        return jnp.where(where, 1.0, 0.0).astype(BF16)

    own = rows[...].astype(BF16)
    r, c = grid((2 * 2 * Z, nrows * 2 * Z))
    near_rows = (c // nrows == r // 2) & (c % nrows == r % 2)
    far_rows = (c // nrows == r // 2) & (c % nrows == nrows - M + r % 2)
    rows_edge[0] = jnp.dot(mark(near_rows), own, preferred_element_type=F32)
    rows_edge[1] = jnp.dot(mark(far_rows), own, preferred_element_type=F32)
    r, c = grid((16, LANE))
    cols_edge[0] = nt_dot(mark((r < M) & (c == r)), colsb[:, 0:LANE])[0:8]
    cols_edge[1] = nt_dot(mark((r < M) & (c == LANE - M + r)), colsb[:, last:ncols])[0:8]
    green_copies = [
        remote(8, rows_edge.at[0], rows_down, (up, py)),
        remote(9, rows_edge.at[1], rows_up, (down, py)),
        remote(10, cols_edge.at[0], cols_right, (px, left)),
        remote(11, cols_edge.at[1], cols_left, (px, right)),
    ]
    share = U // npx
    er = lax.broadcasted_iota(jnp.int32, (4 * U, U), 0)
    ec = lax.broadcasted_iota(jnp.int32, (4 * U, U), 1)
    pick = jnp.where((er // (4 * share)) * share + er % share == ec, 1.0, 0.0).astype(BF16)
    wr = lax.broadcasted_iota(jnp.int32, (U, U), 0)
    placed = jnp.where(wr == order[...], 1.0, 0.0).astype(BF16)
    pick = nt_dot(pick, placed).astype(BF16)

    first_up, last_down = px == 0, px == npx - 1
    first_left, last_right = py == 0, py == npy - 1
    ids = lax.broadcasted_iota(jnp.int32, (LEVELS, ncols), 0)

    def place(at, body, outside):
        n = body.shape[0]
        lane = lax.broadcasted_iota(jnp.int32, (n, LANE), 1)
        side = jnp.where(
            lane < 64,
            jnp.where(last_right, -1, lv_right[at : at + n, :]),
            jnp.where(first_left, -1, lv_left[at : at + n, :]),
        )
        whole = jnp.concatenate([body, side], axis=1)
        if outside is not None:
            whole = jnp.where(outside, -1, whole)
        lvr[0, at : at + n, :] = pltpu.roll(whole, 1, 1)[:, :ncols]
        lvr[1, at : at + n, :] = whole[:, :ncols]
        lvr[2, at : at + n, :] = pltpu.roll(whole, wide - 1, 1)[:, :ncols]

    def encode(i):
        for b in range(3):
            row = lvr[b, 7 + i : 8 + i, :]
            match = jnp.where(ids == row, 1.0, 0.0).astype(BF16)
            onehot[(3 * i + b) * LEVELS : (3 * i + b + 1) * LEVELS, :] = match

    def group(g):
        parts = []
        for r in range(2):
            first = 96 * (2 * g + r)
            act = jnp.dot(w1b, onehot[first : first + 192, :], preferred_element_type=F32) + bias1
            parts.append(gelu(act).astype(BF16))
        hidden = jnp.concatenate(parts, axis=0)
        act = jnp.dot(w2b, hidden, preferred_element_type=F32) + bias2
        features = gelu(act).astype(BF16)
        return jnp.dot(wdb, features, preferred_element_type=F32)

    for copy in side_copies:
        copy.wait()
    place(8, lv[...], None)
    for i in range(1, nrows + 1):
        encode(i)
    tap = group(1)
    taps[160:480, :] = tap
    tap = group(2)
    taps[320:480, :] += tap[0:160]
    taps[480:640, :] = tap[160:320]
    for copy in edge_copies:
        copy.wait()
    place(0, lvx[0:8, :], first_up)
    place(24, lvx[8:16, :], last_down)
    encode(0)
    encode(nrows + 1)
    tap = group(0)
    taps[0:160, :] = tap[0:160]
    taps[160:320, :] += tap[160:320]
    tap = group(3)
    taps[480:640, :] += tap[0:160]
    taps[640:800, :] = tap[160:320]

    for copy in green_copies:
        copy.wait()
    edge = jnp.concatenate(
        [jnp.where(last_right, 0.0, cols_right[...]), jnp.where(first_left, 0.0, cols_left[...])], axis=0
    )
    r, c = grid((16, LANE))
    target = mark(((r < M) & (c == r)) | ((r >= 8) & (r < 8 + M) & (c == LANE - M - 8 + r)))
    colsb[:, ncols:wide] = jnp.dot(edge.T.astype(BF16), target, preferred_element_type=F32).astype(BF16)

    edge = jnp.concatenate(
        [jnp.where(first_up, 0.0, rows_up[...]), jnp.where(last_down, 0.0, rows_down[...])], axis=0
    ).astype(BF16)
    r, c = grid((nrows * 2 * Z, 4 * 2 * Z))
    above = (c < 4 * Z) & (r // nrows == c // 2) & (r % nrows == nrows - M + c % 2)
    below = (c >= 4 * Z) & (r // nrows == c // 2 - 2 * Z) & (r % nrows == c % 2)
    mixed = jnp.dot(mark(above | below), edge, preferred_element_type=F32).astype(BF16)
    pr = (lax.broadcasted_iota(jnp.int32, (4 * U, 2 * LANE), 0) // share) % 4
    pc = (lax.broadcasted_iota(jnp.int32, (4 * U, 2 * LANE), 1) // 32) % 4
    for z in range(Z):
        blocks = []
        for k in range(2):
            at = 32 * z + 16 * k
            blocks += [own[at : at + 16], mixed[at : at + 16]] * 4
        spread = nt_dot(pick, jnp.concatenate(blocks, axis=0))
        lhs[z] = jnp.where(pr == pc, spread, 0.0).astype(BF16)

    blank = jnp.zeros((CH, LANE), F32)
    tiles = []
    for e in range(ext):
        total = None
        for s in range(KS):
            piece = jnp.concatenate([taps[40 * e + 8 * s : 40 * e + 8 * s + 8, :], blank], axis=1)
            if s != M:
                piece = pltpu.roll(piece, (s - M) % wide, 1)
            total = piece if total is None else total + piece
        tiles.append(total)
    near_field = jnp.concatenate(tiles, axis=0).astype(BF16)
    pr = lax.broadcasted_iota(jnp.int32, (CH * 32, CH * ext), 0)
    pc = lax.broadcasted_iota(jnp.int32, (CH * 32, CH * ext), 1)
    perm = jnp.where((pr // 32 == pc % 8) & ((pc // 8 + 30) % 32 == pr % 32), 1.0, 0.0).astype(BF16)
    near_field = jnp.dot(perm, near_field, preferred_element_type=F32).astype(BF16)

    def planes(c):
        cut = pl.ds(pl.multiple_of(256 * c, 256), 256)
        sums = nt_dot(colsb[cut, :], near_field)
        fields = []
        for z in range(2):
            one = sums[LANE * z : LANE * z + LANE, 0:LANE]
            two = sums[LANE * z : LANE * z + LANE, LANE : 2 * LANE]
            real = one[0:64] - two[64:128]
            imag = one[64:128] + two[0:64]
            first = jnp.concatenate([real, imag], axis=0)
            second = jnp.concatenate([-imag, real], axis=0)
            value = jnp.concatenate([first, second], axis=1)
            high = value.astype(BF16)
            low = (value - high.astype(F32)).astype(BF16)
            left_side = lhs[2 * c + z]
            fields.append(nt_dot(left_side, high) + nt_dot(left_side, low))
        return fields

    if not scatter:
        for c in range(Z // 2):
            out[2 * c], out[2 * c + 1] = planes(c)
        return

    def exchange(slot, src, dst, device):
        copy = pltpu.make_async_remote_copy(
            src_ref=src, dst_ref=dst, send_sem=rs_send.at[slot], recv_sem=rs_recv.at[slot],
            device_id=device, device_id_type=MESH,
        )
        copy.start()
        return copy

    core = []
    for i in range(2):
        for z, value in enumerate(planes(2 * (1 - py) + i)):
            field[i, z] = value.reshape(field.shape[2:])
        core.append(exchange(i, field.at[i], r0.at[i], (px, 1 - py)))
    step1 = []
    for i in range(2):
        values = planes(2 * py + i)
        core[i].wait()
        for z in range(2):
            a0[i, z] = values[z].reshape(field.shape[2:]) + r0[i, z]
        step1.append((
            exchange(2 + 7 * i, a0.at[i, 0, :, :, 1 - xq], r1a.at[i], xdev),
            exchange(3 + 7 * i, a0.at[i, 1, :, 1 - yq], r1b.at[i], ydev),
        ))
    step2 = []
    for i in range(2):
        step1[i][0].wait()
        a1a[i] = a0[i, 0, :, :, xq] + r1a[i]
        da = exchange(4 + 7 * i, a1a.at[i, :, 1 - yq], r2a.at[i], ydev)
        step1[i][1].wait()
        a1b[i] = a0[i, 1, :, yq] + r1b[i]
        db = exchange(5 + 7 * i, a1b.at[i, :, 1 - xq], r2b.at[i], xdev)
        step2.append((da, db))
    step3 = []
    for i in range(2):
        step2[i][0].wait()
        a2[i, :, 0] = a1a[i, :, yq] + r2a[i]
        step2[i][1].wait()
        a2[i, :, 1] = a1b[i, :, xq] + r2b[i]
        step3.append([
            exchange(6 + 7 * i + d, a2.at[i, lax.rem(zq + d + 1, 4)], r3.at[i, d], zdevs[d])
            for d in range(3)
        ])
    first_half = lax.broadcasted_iota(jnp.int32, (share, LANE), 1) < 64
    for i in range(2):
        result = a2[i, zq]
        for d, copy in enumerate(step3[i]):
            copy.wait()
            result = result + r3[i, d]
        for z in range(2):
            reals, imags = [], []
            for j in range(2):
                even = result[z, 2 * j * share : (2 * j + 1) * share]
                odd = result[z, (2 * j + 1) * share : (2 * j + 2) * share]
                reals.append(jnp.where(first_half, even, pltpu.roll(odd, 64, 1)))
                imags.append(jnp.where(first_half, pltpu.roll(even, 64, 1), odd))
            out[2 * i + z] = jnp.concatenate(reals + imags, axis=1)


def on_device(
    levels, conv_table, conv_bias, mix_weight, mix_bias, decoder, green_rows, green_cols, focal_order
):
    npx = lax.axis_size("px")
    npy = lax.axis_size("py")
    nrows, ncols = levels.shape
    wide = ncols + LANE
    scatter = npx == 16 and npy == 2
    width = CH * V
    share = U // npx
    rows = green_rows.transpose(0, 1, 3, 2).reshape(Z * 2 * nrows, U)
    cols = green_cols.reshape(Z * 2 * V, ncols)
    operands = (
        levels, conv_table, conv_bias.reshape(1, HID), mix_weight, mix_bias.reshape(1, HID),
        decoder, rows, cols, focal_order.reshape(1, U),
    )

    def rs(*shape):
        return pltpu.VMEM(shape if scatter else (8, LANE), F32)

    def like(array):
        return pltpu.VMEM(array.shape, array.dtype)

    result = pl.pallas_call(
        functools.partial(kernel, npx, npy, scatter),
        out_shape=jax.ShapeDtypeStruct((Z // npy, share, width) if scatter else (Z, 4 * U, 2 * V), F32),
        in_specs=[pl.BlockSpec(memory_space=pltpu.HBM)] * 9,
        out_specs=pl.BlockSpec(memory_space=pltpu.VMEM),
        scratch_shapes=[
            *[like(operands[i]) for i in (0, 1, 2, 3, 4, 5, 6, 8)],
            pltpu.VMEM((16, ncols), jnp.int32),
            pltpu.VMEM((32, LANE), jnp.int32),
            pltpu.VMEM((32, LANE), jnp.int32),
            pltpu.VMEM((3, 32, ncols), jnp.int32),
            pltpu.VMEM(((nrows + 2) * 3 * LEVELS, ncols), BF16),
            pltpu.VMEM((2 * HID, 192), F32),
            pltpu.VMEM((4 * HID, 4 * HID), F32),
            pltpu.VMEM((8 * KS * CH, 4 * HID), F32),
            pltpu.VMEM(((nrows + 2 * M) * KS * CH, ncols), F32),
            pltpu.VMEM(cols.shape, F32),
            pltpu.VMEM((8, cols.shape[0]), F32),
            pltpu.VMEM((8, cols.shape[0]), F32),
            pltpu.VMEM((cols.shape[0], wide), BF16),
            pltpu.VMEM((4 * Z, U), F32),
            pltpu.VMEM((4 * Z, U), F32),
            pltpu.VMEM((2, 4 * Z, U), F32),
            pltpu.VMEM((2, 8, cols.shape[0]), F32),
            pltpu.VMEM((Z, 4 * U, 2 * LANE), BF16),
            rs(2, 2, 4, 2, 2, 16, LANE),
            rs(2, 2, 4, 2, 2, 16, LANE),
            rs(2, 2, 4, 2, 2, 16, LANE),
            rs(2, 4, 2, 16, LANE),
            rs(2, 4, 2, 16, LANE),
            rs(2, 4, 2, 16, LANE),
            rs(2, 4, 2, 16, LANE),
            rs(2, 4, 16, LANE),
            rs(2, 4, 16, LANE),
            rs(2, 4, 2, 16, LANE),
            rs(2, 3, 2, 16, LANE),
            pltpu.SemaphoreType.DMA((12,)),
            pltpu.SemaphoreType.DMA((12,)),
            pltpu.SemaphoreType.DMA((16,)),
            pltpu.SemaphoreType.DMA((16,)),
            pltpu.SemaphoreType.DMA((9,)),
        ],
        compiler_params=pltpu.CompilerParams(
            collective_id=0, has_side_effects=True, vmem_limit_bytes=56 * 1024 * 1024
        ),
    )(*operands)
    if scatter:
        return result
    result = result.reshape(Z, npx, 4 * share, 2 * V).transpose(1, 0, 2, 3)
    own = lax.psum_scatter(
        result.reshape(npx * Z, 4 * share * 2 * V), ("px", "py"), scatter_dimension=0, tiled=True
    )
    own = own.reshape(Z // npy, CH // 2, share, 2, V).transpose(0, 2, 3, 1, 4)
    return own.reshape(Z // npy, share, width)


def solution(mesh):
    return jax.shard_map(
        on_device,
        mesh=mesh,
        in_specs=(
            P("px", "py"),
            P(),
            P(),
            P(),
            P(),
            P(),
            P(None, None, None, "px"),
            P(None, None, None, "py"),
            P(),
        ),
        out_specs=P("py", "px", None),
        check_vma=False,
    )
```

```python
import functools

import jax
import jax.numpy as jnp
from jax import lax
from jax.experimental import pallas as pl
from jax.experimental.pallas import tpu as pltpu
from jax.sharding import PartitionSpec as P

CH = 8
M = 2
KS = 5
Z = 8
U = 64
V = 64
LEVELS = 16
HID = 64
LANE = 128
MESH = pl.DeviceIdType.MESH
F32 = jnp.float32
BF16 = jnp.bfloat16


def gelu(half):
    inner = half * (1.5957691216057308 + (1.5957691216057308 * 4 * 0.044715) * (half * half))
    return half + half * jnp.tanh(inner)


def column(row):
    n = row.shape[1]
    here = lax.broadcasted_iota(jnp.int32, (n, n), 0) == lax.broadcasted_iota(jnp.int32, (n, n), 1)
    return jnp.sum(jnp.where(here, row, 0.0), axis=1, keepdims=True)


def nt_dot(a, b):
    return lax.dot_general(a, b, (((1,), (1,)), ((), ())), preferred_element_type=F32)


def kernel(
    npx, npy, scatter,
    lv_in, table_in, cb_in, mix_in, mb_in, dec_in, rows_in, cols_in, order_in, out,
    lv, table, conv_bias, mix, mix_bias, dec, rows, order,
    lvx, lv_right, lv_left, lvr, onehot, w1, w2, wd, taps, cols, cols_right, cols_left, colsb,
    rows_up, rows_down, rows_edge, cols_edge, near_t, lhs, field, r0, a0, r1a, r1b, a1a, a1b, r2a, r2b, a2, r3,
    send, recv, rs_send, rs_recv, load_sem,
):
    px = lax.axis_index("px")
    py = lax.axis_index("py")
    nrows, ncols = lv.shape
    wide = ncols + LANE
    ext = nrows + 2 * M

    up, down = lax.rem(px + npx - 1, npx), lax.rem(px + 1, npx)
    left, right = lax.rem(py + npy - 1, npy), lax.rem(py + 1, npy)
    greeted = [
        (up, py), (down, py), (px, left), (px, right),
        (up, left), (up, right), (down, left), (down, right),
    ]
    if scatter:
        xq = lax.rem(px, 2)
        yq = lax.rem(px // 2, 2)
        zq = px // 4
        xdev = (px + 1 - 2 * xq, py)
        ydev = (px + 2 - 4 * yq, py)
        zdevs = [(lax.rem(px + 4 * d, 16), py) for d in (1, 2, 3)]
        greeted += [xdev, ydev] + zdevs

    barrier = pltpu.get_barrier_semaphore()
    for device in greeted:
        pl.semaphore_signal(barrier, inc=1, device_id=device, device_id_type=MESH)
    loads = []
    for i, (src, dst) in enumerate([
        (table_in, table), (cb_in, conv_bias), (mix_in, mix), (mb_in, mix_bias), (dec_in, dec),
        (lv_in, lv), (rows_in, rows), (order_in, order), (cols_in, cols),
    ]):
        loads.append(pltpu.make_async_copy(src, dst, load_sem.at[i]))
        loads[-1].start()
    for load in loads[:5]:
        load.wait()

    w1[...] = jnp.zeros_like(w1)
    for r in range(2):
        w1[HID * r : HID * (r + 1), 48 * r : 48 * r + 144] = 0.5 * table[...].astype(F32)
    w2[...] = jnp.zeros_like(w2)
    for r in range(4):
        w2[HID * r : HID * (r + 1), HID * r : HID * (r + 1)] = 0.5 * mix[...].astype(F32)
    wd[...] = jnp.zeros_like(wd)
    for r in range(4):
        for t in range(KS):
            e = r + t
            wd[40 * e : 40 * (e + 1), HID * r : HID * (r + 1)] = dec[t].astype(F32)
    w1b = w1[...].astype(BF16)
    w2b = w2[...].astype(BF16)
    wdb = wd[...].astype(BF16)
    bias1 = column(0.5 * conv_bias[...])
    bias1 = jnp.concatenate([bias1, bias1], axis=0)
    bias2 = column(0.5 * mix_bias[...])
    bias2 = jnp.concatenate([bias2] * 4, axis=0)

    last = ncols - LANE
    for load in loads[5:]:
        load.wait()
    colsb[:, 0:ncols] = cols[...].astype(BF16)

    def grid(shape):
        return lax.broadcasted_iota(jnp.int32, shape, 0), lax.broadcasted_iota(jnp.int32, shape, 1)

    def mark(where):
        return jnp.where(where, 1.0, 0.0).astype(BF16)

    own = rows[...].astype(BF16)
    r, c = grid((2 * 2 * Z, nrows * 2 * Z))
    near_rows = (c // nrows == r // 2) & (c % nrows == r % 2)
    far_rows = (c // nrows == r // 2) & (c % nrows == nrows - M + r % 2)
    rows_edge[0] = jnp.dot(mark(near_rows), own, preferred_element_type=F32)
    rows_edge[1] = jnp.dot(mark(far_rows), own, preferred_element_type=F32)
    r, c = grid((16, LANE))
    cols_edge[0] = nt_dot(mark((r < M) & (c == r)), colsb[:, 0:LANE])[0:8]
    cols_edge[1] = nt_dot(mark((r < M) & (c == LANE - M + r)), colsb[:, last:ncols])[0:8]
    share = U // npx
    er = lax.broadcasted_iota(jnp.int32, (4 * U, U), 0)
    ec = lax.broadcasted_iota(jnp.int32, (4 * U, U), 1)
    pick = jnp.where((er // (4 * share)) * share + er % share == ec, 1.0, 0.0).astype(BF16)
    wr = lax.broadcasted_iota(jnp.int32, (U, U), 0)
    placed = jnp.where(wr == order[...], 1.0, 0.0).astype(BF16)
    pick = nt_dot(pick, placed).astype(BF16)

    pl.semaphore_wait(barrier, len(greeted))

    def remote(slot, src, dst, device):
        copy = pltpu.make_async_remote_copy(
            src_ref=src, dst_ref=dst, send_sem=send.at[slot], recv_sem=recv.at[slot],
            device_id=device, device_id_type=MESH,
        )
        copy.start()
        return copy

    side_copies = [
        remote(0, lv_in.at[:, 0:LANE], lv_right.at[8:24, :], (px, left)),
        remote(1, lv_in.at[:, last:ncols], lv_left.at[8:24, :], (px, right)),
    ]
    edge_copies = [
        remote(2, lv_in.at[nrows - 8 : nrows, :], lvx.at[0:8, :], (down, py)),
        remote(3, lv_in.at[0:8, :], lvx.at[8:16, :], (up, py)),
        remote(4, lv_in.at[nrows - 8 : nrows, 0:LANE], lv_right.at[0:8, :], (down, left)),
        remote(5, lv_in.at[nrows - 8 : nrows, last:ncols], lv_left.at[0:8, :], (down, right)),
        remote(6, lv_in.at[0:8, 0:LANE], lv_right.at[24:32, :], (up, left)),
        remote(7, lv_in.at[0:8, last:ncols], lv_left.at[24:32, :], (up, right)),
    ]
    green_copies = [
        remote(8, rows_edge.at[0], rows_down, (up, py)),
        remote(9, rows_edge.at[1], rows_up, (down, py)),
        remote(10, cols_edge.at[0], cols_right, (px, left)),
        remote(11, cols_edge.at[1], cols_left, (px, right)),
    ]

    first_up, last_down = px == 0, px == npx - 1
    first_left, last_right = py == 0, py == npy - 1
    ids = lax.broadcasted_iota(jnp.int32, (LEVELS, ncols), 0)

    def place(at, body, outside):
        n = body.shape[0]
        lane = lax.broadcasted_iota(jnp.int32, (n, LANE), 1)
        side = jnp.where(
            lane < 64,
            jnp.where(last_right, -1, lv_right[at : at + n, :]),
            jnp.where(first_left, -1, lv_left[at : at + n, :]),
        )
        whole = jnp.concatenate([body, side], axis=1)
        if outside is not None:
            whole = jnp.where(outside, -1, whole)
        lvr[0, at : at + n, :] = pltpu.roll(whole, 1, 1)[:, :ncols]
        lvr[1, at : at + n, :] = whole[:, :ncols]
        lvr[2, at : at + n, :] = pltpu.roll(whole, wide - 1, 1)[:, :ncols]

    def encode(i):
        for b in range(3):
            row = lvr[b, 7 + i : 8 + i, :]
            match = jnp.where(ids == row, 1.0, 0.0).astype(BF16)
            onehot[(3 * i + b) * LEVELS : (3 * i + b + 1) * LEVELS, :] = match

    def group(g):
        parts = []
        for r in range(2):
            first = 96 * (2 * g + r)
            act = jnp.dot(w1b, onehot[first : first + 192, :], preferred_element_type=F32) + bias1
            parts.append(gelu(act).astype(BF16))
        hidden = jnp.concatenate(parts, axis=0)
        act = jnp.dot(w2b, hidden, preferred_element_type=F32) + bias2
        features = gelu(act).astype(BF16)
        return jnp.dot(wdb, features, preferred_element_type=F32)

    for copy in side_copies:
        copy.wait()
    place(8, lv[...], None)
    for i in range(1, nrows + 1):
        encode(i)
    tap = group(1)
    taps[160:480, :] = tap
    tap = group(2)
    taps[320:480, :] += tap[0:160]
    taps[480:640, :] = tap[160:320]
    for copy in edge_copies:
        copy.wait()
    place(0, lvx[0:8, :], first_up)
    place(24, lvx[8:16, :], last_down)
    encode(0)
    encode(nrows + 1)
    tap = group(0)
    taps[0:160, :] = tap[0:160]
    taps[160:320, :] += tap[160:320]
    tap = group(3)
    taps[480:640, :] += tap[0:160]
    taps[640:800, :] = tap[160:320]

    for copy in green_copies:
        copy.wait()
    edge = jnp.concatenate(
        [jnp.where(last_right, 0.0, cols_right[...]), jnp.where(first_left, 0.0, cols_left[...])], axis=0
    )
    r, c = grid((16, LANE))
    target = mark(((r < M) & (c == r)) | ((r >= 8) & (r < 8 + M) & (c == LANE - M - 8 + r)))
    colsb[:, ncols:wide] = jnp.dot(edge.T.astype(BF16), target, preferred_element_type=F32).astype(BF16)

    edge = jnp.concatenate(
        [jnp.where(first_up, 0.0, rows_up[...]), jnp.where(last_down, 0.0, rows_down[...])], axis=0
    ).astype(BF16)
    r, c = grid((nrows * 2 * Z, 4 * 2 * Z))
    above = (c < 4 * Z) & (r // nrows == c // 2) & (r % nrows == nrows - M + c % 2)
    below = (c >= 4 * Z) & (r // nrows == c // 2 - 2 * Z) & (r % nrows == c % 2)
    mixed = jnp.dot(mark(above | below), edge, preferred_element_type=F32).astype(BF16)
    pr = (lax.broadcasted_iota(jnp.int32, (4 * U, 2 * LANE), 0) // share) % 4
    pc = (lax.broadcasted_iota(jnp.int32, (4 * U, 2 * LANE), 1) // 32) % 4
    for z in range(Z):
        blocks = []
        for k in range(2):
            at = 32 * z + 16 * k
            blocks += [own[at : at + 16], mixed[at : at + 16]] * 4
        spread = nt_dot(pick, jnp.concatenate(blocks, axis=0))
        lhs[z] = jnp.where(pr == pc, spread, 0.0).astype(BF16)

    blank = jnp.zeros((CH, LANE), F32)
    tiles = []
    for e in range(ext):
        total = None
        for s in range(KS):
            piece = jnp.concatenate([taps[40 * e + 8 * s : 40 * e + 8 * s + 8, :], blank], axis=1)
            if s != M:
                piece = pltpu.roll(piece, (s - M) % wide, 1)
            total = piece if total is None else total + piece
        tiles.append(total)
    near_field = jnp.concatenate(tiles, axis=0).astype(BF16)
    pr = lax.broadcasted_iota(jnp.int32, (CH * 32, CH * ext), 0)
    pc = lax.broadcasted_iota(jnp.int32, (CH * 32, CH * ext), 1)
    perm = jnp.where((pr // 32 == pc % 8) & ((pc // 8 + 30) % 32 == pr % 32), 1.0, 0.0).astype(BF16)
    near_t[...] = jnp.dot(perm, near_field, preferred_element_type=F32).T.astype(BF16)

    def planes(c):
        cut = pl.ds(pl.multiple_of(256 * c, 256), 256)
        sums = jnp.dot(colsb[cut, :], near_t[...], preferred_element_type=F32)
        fields = []
        for z in range(2):
            one = sums[LANE * z : LANE * z + LANE, 0:LANE]
            two = sums[LANE * z : LANE * z + LANE, LANE : 2 * LANE]
            real = one[0:64] - two[64:128]
            imag = one[64:128] + two[0:64]
            first = jnp.concatenate([real, imag], axis=0)
            second = jnp.concatenate([-imag, real], axis=0)
            value = jnp.concatenate([first, second], axis=1)
            high = value.astype(BF16)
            low = (value - high.astype(F32)).astype(BF16)
            left_side = lhs[2 * c + z]
            both = nt_dot(left_side, jnp.concatenate([high, low], axis=0))
            fields.append(both[:, 0:LANE] + both[:, LANE : 2 * LANE])
        return fields

    if not scatter:
        for c in range(Z // 2):
            out[2 * c], out[2 * c + 1] = planes(c)
        return

    def exchange(slot, src, dst, device):
        copy = pltpu.make_async_remote_copy(
            src_ref=src, dst_ref=dst, send_sem=rs_send.at[slot], recv_sem=rs_recv.at[slot],
            device_id=device, device_id_type=MESH,
        )
        copy.start()
        return copy

    core = []
    for i in range(2):
        for z, value in enumerate(planes(2 * (1 - py) + i)):
            field[i, z] = value.reshape(field.shape[2:])
        core.append(exchange(i, field.at[i], r0.at[i], (px, 1 - py)))
    step1 = []
    for i in range(2):
        values = planes(2 * py + i)
        core[i].wait()
        for z in range(2):
            a0[i, z] = values[z].reshape(field.shape[2:]) + r0[i, z]
        step1.append((
            exchange(2 + 7 * i, a0.at[i, 0, :, :, 1 - xq], r1a.at[i], xdev),
            exchange(3 + 7 * i, a0.at[i, 1, :, 1 - yq], r1b.at[i], ydev),
        ))
    step2 = []
    for i in range(2):
        step1[i][0].wait()
        a1a[i] = a0[i, 0, :, :, xq] + r1a[i]
        da = exchange(4 + 7 * i, a1a.at[i, :, 1 - yq], r2a.at[i], ydev)
        step1[i][1].wait()
        a1b[i] = a0[i, 1, :, yq] + r1b[i]
        db = exchange(5 + 7 * i, a1b.at[i, :, 1 - xq], r2b.at[i], xdev)
        step2.append((da, db))
    step3 = []
    for i in range(2):
        step2[i][0].wait()
        a2[i, :, 0] = a1a[i, :, yq] + r2a[i]
        step2[i][1].wait()
        a2[i, :, 1] = a1b[i, :, xq] + r2b[i]
        step3.append([
            exchange(6 + 7 * i + d, a2.at[i, lax.rem(zq + d + 1, 4)], r3.at[i, d], zdevs[d])
            for d in range(3)
        ])
    first_half = lax.broadcasted_iota(jnp.int32, (share, LANE), 1) < 64
    for i in range(2):
        result = a2[i, zq]
        for d, copy in enumerate(step3[i]):
            copy.wait()
            result = result + r3[i, d]
        for z in range(2):
            reals, imags = [], []
            for j in range(2):
                even = result[z, 2 * j * share : (2 * j + 1) * share]
                odd = result[z, (2 * j + 1) * share : (2 * j + 2) * share]
                reals.append(jnp.where(first_half, even, pltpu.roll(odd, 64, 1)))
                imags.append(jnp.where(first_half, pltpu.roll(even, 64, 1), odd))
            out[2 * i + z] = jnp.concatenate(reals + imags, axis=1)


def on_device(
    levels, conv_table, conv_bias, mix_weight, mix_bias, decoder, green_rows, green_cols, focal_order
):
    npx = lax.axis_size("px")
    npy = lax.axis_size("py")
    nrows, ncols = levels.shape
    wide = ncols + LANE
    scatter = npx == 16 and npy == 2
    width = CH * V
    share = U // npx
    rows = green_rows.transpose(0, 1, 3, 2).reshape(Z * 2 * nrows, U)
    cols = green_cols.reshape(Z * 2 * V, ncols)
    operands = (
        levels, conv_table, conv_bias.reshape(1, HID), mix_weight, mix_bias.reshape(1, HID),
        decoder, rows, cols, focal_order.reshape(1, U),
    )

    def rs(*shape):
        return pltpu.VMEM(shape if scatter else (8, LANE), F32)

    def like(array):
        return pltpu.VMEM(array.shape, array.dtype)

    result = pl.pallas_call(
        functools.partial(kernel, npx, npy, scatter),
        out_shape=jax.ShapeDtypeStruct((Z // npy, share, width) if scatter else (Z, 4 * U, 2 * V), F32),
        in_specs=[pl.BlockSpec(memory_space=pltpu.HBM)] * 9,
        out_specs=pl.BlockSpec(memory_space=pltpu.VMEM),
        scratch_shapes=[
            *[like(operands[i]) for i in (0, 1, 2, 3, 4, 5, 6, 8)],
            pltpu.VMEM((16, ncols), jnp.int32),
            pltpu.VMEM((32, LANE), jnp.int32),
            pltpu.VMEM((32, LANE), jnp.int32),
            pltpu.VMEM((3, 32, ncols), jnp.int32),
            pltpu.VMEM(((nrows + 2) * 3 * LEVELS, ncols), BF16),
            pltpu.VMEM((2 * HID, 192), F32),
            pltpu.VMEM((4 * HID, 4 * HID), F32),
            pltpu.VMEM((8 * KS * CH, 4 * HID), F32),
            pltpu.VMEM(((nrows + 2 * M) * KS * CH, ncols), F32),
            pltpu.VMEM(cols.shape, F32),
            pltpu.VMEM((8, cols.shape[0]), F32),
            pltpu.VMEM((8, cols.shape[0]), F32),
            pltpu.VMEM((cols.shape[0], wide), BF16),
            pltpu.VMEM((4 * Z, U), F32),
            pltpu.VMEM((4 * Z, U), F32),
            pltpu.VMEM((2, 4 * Z, U), F32),
            pltpu.VMEM((2, 8, cols.shape[0]), F32),
            pltpu.VMEM((wide, CH * 32), BF16),
            pltpu.VMEM((Z, 4 * U, 2 * LANE), BF16),
            rs(2, 2, 4, 2, 2, 16, LANE),
            rs(2, 2, 4, 2, 2, 16, LANE),
            rs(2, 2, 4, 2, 2, 16, LANE),
            rs(2, 4, 2, 16, LANE),
            rs(2, 4, 2, 16, LANE),
            rs(2, 4, 2, 16, LANE),
            rs(2, 4, 2, 16, LANE),
            rs(2, 4, 16, LANE),
            rs(2, 4, 16, LANE),
            rs(2, 4, 2, 16, LANE),
            rs(2, 3, 2, 16, LANE),
            pltpu.SemaphoreType.DMA((12,)),
            pltpu.SemaphoreType.DMA((12,)),
            pltpu.SemaphoreType.DMA((16,)),
            pltpu.SemaphoreType.DMA((16,)),
            pltpu.SemaphoreType.DMA((9,)),
        ],
        compiler_params=pltpu.CompilerParams(
            collective_id=0, has_side_effects=True, vmem_limit_bytes=56 * 1024 * 1024
        ),
    )(*operands)
    if scatter:
        return result
    result = result.reshape(Z, npx, 4 * share, 2 * V).transpose(1, 0, 2, 3)
    own = lax.psum_scatter(
        result.reshape(npx * Z, 4 * share * 2 * V), ("px", "py"), scatter_dimension=0, tiled=True
    )
    own = own.reshape(Z // npy, CH // 2, share, 2, V).transpose(0, 2, 3, 1, 4)
    return own.reshape(Z // npy, share, width)


def solution(mesh):
    return jax.shard_map(
        on_device,
        mesh=mesh,
        in_specs=(
            P("px", "py"),
            P(),
            P(),
            P(),
            P(),
            P(),
            P(None, None, None, "px"),
            P(None, None, None, "py"),
            P(),
        ),
        out_specs=P("py", "px", None),
        check_vma=False,
    )
```

```python
import functools

import jax
import jax.numpy as jnp
from jax import lax
from jax.experimental import pallas as pl
from jax.experimental.pallas import tpu as pltpu
from jax.sharding import PartitionSpec as P

CH = 8
M = 2
KS = 5
Z = 8
U = 64
V = 64
LEVELS = 16
HID = 64
LANE = 128
MESH = pl.DeviceIdType.MESH
F32 = jnp.float32
BF16 = jnp.bfloat16


def gelu(half):
    inner = half * (1.5957691216057308 + (1.5957691216057308 * 4 * 0.044715) * (half * half))
    return half + half * jnp.tanh(inner)


def column(row):
    n = row.shape[1]
    here = lax.broadcasted_iota(jnp.int32, (n, n), 0) == lax.broadcasted_iota(jnp.int32, (n, n), 1)
    return jnp.sum(jnp.where(here, row, 0.0), axis=1, keepdims=True)


def nt_dot(a, b):
    return lax.dot_general(a, b, (((1,), (1,)), ((), ())), preferred_element_type=F32)


def kernel(
    npx, npy, scatter,
    lv_in, table_in, cb_in, mix_in, mb_in, dec_in, rows_in, cols_in, order_in, out,
    lv, table, conv_bias, mix, mix_bias, dec, rows, order,
    lvx, lv_right, lv_left, lvr, onehot, w1, w2, wd, taps, cols, cols_right, cols_left, colsb,
    rows_up, rows_down, rows_edge, cols_edge, near_t, lhs, field, r0, a0, r1a, r1b, r1h, a1a, a1b, a1h, r2a, r2b, r2h, a2, r3, rz, c1, c2, rcx, rcy,
    send, recv, rs_send, rs_recv, load_sem,
):
    px = lax.axis_index("px")
    py = lax.axis_index("py")
    nrows, ncols = lv.shape
    wide = ncols + LANE
    ext = nrows + 2 * M

    up, down = lax.rem(px + npx - 1, npx), lax.rem(px + 1, npx)
    left, right = lax.rem(py + npy - 1, npy), lax.rem(py + 1, npy)
    greeted = [
        (up, py), (down, py), (px, left), (px, right),
        (up, left), (up, right), (down, left), (down, right),
    ]
    if scatter:
        xq = lax.rem(px, 2)
        yq = lax.rem(px // 2, 2)
        zq = px // 4
        xdev = (px + 1 - 2 * xq, py)
        ydev = (px + 2 - 4 * yq, py)
        zdevs = [(lax.rem(px + 4 * d, 16), py) for d in (1, 2, 3)]
        greeted += [xdev, ydev] + zdevs

    barrier = pltpu.get_barrier_semaphore()
    for device in greeted:
        pl.semaphore_signal(barrier, inc=1, device_id=device, device_id_type=MESH)
    loads = []
    for i, (src, dst) in enumerate([
        (table_in, table), (cb_in, conv_bias), (mix_in, mix), (mb_in, mix_bias), (dec_in, dec),
        (lv_in, lv), (rows_in, rows), (order_in, order), (cols_in, cols),
    ]):
        loads.append(pltpu.make_async_copy(src, dst, load_sem.at[i]))
        loads[-1].start()
    for load in loads[:5]:
        load.wait()

    w1[...] = jnp.zeros_like(w1)
    for r in range(2):
        w1[HID * r : HID * (r + 1), 48 * r : 48 * r + 144] = 0.5 * table[...].astype(F32)
    w2[...] = jnp.zeros_like(w2)
    for r in range(4):
        w2[HID * r : HID * (r + 1), HID * r : HID * (r + 1)] = 0.5 * mix[...].astype(F32)
    wd[...] = jnp.zeros_like(wd)
    for r in range(4):
        for t in range(KS):
            e = r + t
            wd[40 * e : 40 * (e + 1), HID * r : HID * (r + 1)] = dec[t].astype(F32)
    w1b = w1[...].astype(BF16)
    w2b = w2[...].astype(BF16)
    wdb = wd[...].astype(BF16)
    bias1 = column(0.5 * conv_bias[...])
    bias1 = jnp.concatenate([bias1, bias1], axis=0)
    bias2 = column(0.5 * mix_bias[...])
    bias2 = jnp.concatenate([bias2] * 4, axis=0)

    last = ncols - LANE
    for load in loads[5:]:
        load.wait()
    colsb[:, 0:ncols] = cols[...].astype(BF16)

    def grid(shape):
        return lax.broadcasted_iota(jnp.int32, shape, 0), lax.broadcasted_iota(jnp.int32, shape, 1)

    def mark(where):
        return jnp.where(where, 1.0, 0.0).astype(BF16)

    own = rows[...].astype(BF16)
    r, c = grid((2 * 2 * Z, nrows * 2 * Z))
    near_rows = (c // nrows == r // 2) & (c % nrows == r % 2)
    far_rows = (c // nrows == r // 2) & (c % nrows == nrows - M + r % 2)
    rows_edge[0] = jnp.dot(mark(near_rows), own, preferred_element_type=F32)
    rows_edge[1] = jnp.dot(mark(far_rows), own, preferred_element_type=F32)
    r, c = grid((16, LANE))
    cols_edge[0] = nt_dot(mark((r < M) & (c == r)), colsb[:, 0:LANE])[0:8]
    cols_edge[1] = nt_dot(mark((r < M) & (c == LANE - M + r)), colsb[:, last:ncols])[0:8]
    share = U // npx
    er = lax.broadcasted_iota(jnp.int32, (4 * U, U), 0)
    ec = lax.broadcasted_iota(jnp.int32, (4 * U, U), 1)
    pick = jnp.where((er // (4 * share)) * share + er % share == ec, 1.0, 0.0).astype(BF16)
    wr = lax.broadcasted_iota(jnp.int32, (U, U), 0)
    placed = jnp.where(wr == order[...], 1.0, 0.0).astype(BF16)
    pick = nt_dot(pick, placed).astype(BF16)

    pl.semaphore_wait(barrier, len(greeted))

    def remote(slot, src, dst, device):
        copy = pltpu.make_async_remote_copy(
            src_ref=src, dst_ref=dst, send_sem=send.at[slot], recv_sem=recv.at[slot],
            device_id=device, device_id_type=MESH,
        )
        copy.start()
        return copy

    side_copies = [
        remote(0, lv_in.at[:, 0:LANE], lv_right.at[8:24, :], (px, left)),
        remote(1, lv_in.at[:, last:ncols], lv_left.at[8:24, :], (px, right)),
    ]
    edge_copies = [
        remote(2, lv_in.at[nrows - 8 : nrows, :], lvx.at[0:8, :], (down, py)),
        remote(3, lv_in.at[0:8, :], lvx.at[8:16, :], (up, py)),
        remote(4, lv_in.at[nrows - 8 : nrows, 0:LANE], lv_right.at[0:8, :], (down, left)),
        remote(5, lv_in.at[nrows - 8 : nrows, last:ncols], lv_left.at[0:8, :], (down, right)),
        remote(6, lv_in.at[0:8, 0:LANE], lv_right.at[24:32, :], (up, left)),
        remote(7, lv_in.at[0:8, last:ncols], lv_left.at[24:32, :], (up, right)),
    ]
    green_copies = [
        remote(8, rows_edge.at[0], rows_down, (up, py)),
        remote(9, rows_edge.at[1], rows_up, (down, py)),
        remote(10, cols_edge.at[0], cols_right, (px, left)),
        remote(11, cols_edge.at[1], cols_left, (px, right)),
    ]

    first_up, last_down = px == 0, px == npx - 1
    first_left, last_right = py == 0, py == npy - 1
    ids = lax.broadcasted_iota(jnp.int32, (LEVELS, ncols), 0)

    def place(at, body, outside):
        n = body.shape[0]
        lane = lax.broadcasted_iota(jnp.int32, (n, LANE), 1)
        side = jnp.where(
            lane < 64,
            jnp.where(last_right, -1, lv_right[at : at + n, :]),
            jnp.where(first_left, -1, lv_left[at : at + n, :]),
        )
        whole = jnp.concatenate([body, side], axis=1)
        if outside is not None:
            whole = jnp.where(outside, -1, whole)
        lvr[0, at : at + n, :] = pltpu.roll(whole, 1, 1)[:, :ncols]
        lvr[1, at : at + n, :] = whole[:, :ncols]
        lvr[2, at : at + n, :] = pltpu.roll(whole, wide - 1, 1)[:, :ncols]

    def encode(i):
        for b in range(3):
            row = lvr[b, 7 + i : 8 + i, :]
            match = jnp.where(ids == row, 1.0, 0.0).astype(BF16)
            onehot[(3 * i + b) * LEVELS : (3 * i + b + 1) * LEVELS, :] = match

    def group(g):
        parts = []
        for r in range(2):
            first = 96 * (2 * g + r)
            act = jnp.dot(w1b, onehot[first : first + 192, :], preferred_element_type=F32) + bias1
            parts.append(gelu(act).astype(BF16))
        hidden = jnp.concatenate(parts, axis=0)
        act = jnp.dot(w2b, hidden, preferred_element_type=F32) + bias2
        features = gelu(act).astype(BF16)
        return jnp.dot(wdb, features, preferred_element_type=F32)

    for copy in side_copies:
        copy.wait()
    place(8, lv[...], None)
    for i in range(1, nrows + 1):
        encode(i)
    tap = group(1)
    taps[160:480, :] = tap
    tap = group(2)
    taps[320:480, :] += tap[0:160]
    taps[480:640, :] = tap[160:320]
    for copy in edge_copies:
        copy.wait()
    place(0, lvx[0:8, :], first_up)
    place(24, lvx[8:16, :], last_down)
    encode(0)
    encode(nrows + 1)
    tap = group(0)
    taps[0:160, :] = tap[0:160]
    taps[160:320, :] += tap[160:320]
    tap = group(3)
    taps[480:640, :] += tap[0:160]
    taps[640:800, :] = tap[160:320]

    for copy in green_copies:
        copy.wait()
    edge = jnp.concatenate(
        [jnp.where(last_right, 0.0, cols_right[...]), jnp.where(first_left, 0.0, cols_left[...])], axis=0
    )
    r, c = grid((16, LANE))
    target = mark(((r < M) & (c == r)) | ((r >= 8) & (r < 8 + M) & (c == LANE - M - 8 + r)))
    colsb[:, ncols:wide] = jnp.dot(edge.T.astype(BF16), target, preferred_element_type=F32).astype(BF16)

    edge = jnp.concatenate(
        [jnp.where(first_up, 0.0, rows_up[...]), jnp.where(last_down, 0.0, rows_down[...])], axis=0
    ).astype(BF16)
    r, c = grid((nrows * 2 * Z, 4 * 2 * Z))
    above = (c < 4 * Z) & (r // nrows == c // 2) & (r % nrows == nrows - M + c % 2)
    below = (c >= 4 * Z) & (r // nrows == c // 2 - 2 * Z) & (r % nrows == c % 2)
    mixed = jnp.dot(mark(above | below), edge, preferred_element_type=F32).astype(BF16)
    pr = (lax.broadcasted_iota(jnp.int32, (4 * U, 2 * LANE), 0) // share) % 4
    pc = (lax.broadcasted_iota(jnp.int32, (4 * U, 2 * LANE), 1) // 32) % 4
    for z in range(Z):
        blocks = []
        for k in range(2):
            at = 32 * z + 16 * k
            blocks += [own[at : at + 16], mixed[at : at + 16]] * 4
        spread = nt_dot(pick, jnp.concatenate(blocks, axis=0))
        lhs[z] = jnp.where(pr == pc, spread, 0.0).astype(BF16)

    blank = jnp.zeros((CH, LANE), F32)
    tiles = []
    for e in range(ext):
        total = None
        for s in range(KS):
            piece = jnp.concatenate([taps[40 * e + 8 * s : 40 * e + 8 * s + 8, :], blank], axis=1)
            if s != M:
                piece = pltpu.roll(piece, (s - M) % wide, 1)
            total = piece if total is None else total + piece
        tiles.append(total)
    near_field = jnp.concatenate(tiles, axis=0).astype(BF16)
    pr = lax.broadcasted_iota(jnp.int32, (CH * 32, CH * ext), 0)
    pc = lax.broadcasted_iota(jnp.int32, (CH * 32, CH * ext), 1)
    perm = jnp.where((pr // 32 == pc % 8) & ((pc // 8 + 30) % 32 == pr % 32), 1.0, 0.0).astype(BF16)
    near_t[...] = jnp.dot(perm, near_field, preferred_element_type=F32).T.astype(BF16)

    def planes(c):
        cut = pl.ds(pl.multiple_of(256 * c, 256), 256)
        sums = jnp.dot(colsb[cut, :], near_t[...], preferred_element_type=F32)
        fields = []
        for z in range(2):
            one = sums[LANE * z : LANE * z + LANE, 0:LANE]
            two = sums[LANE * z : LANE * z + LANE, LANE : 2 * LANE]
            real = one[0:64] - two[64:128]
            imag = one[64:128] + two[0:64]
            first = jnp.concatenate([real, imag], axis=0)
            second = jnp.concatenate([-imag, real], axis=0)
            value = jnp.concatenate([first, second], axis=1)
            high = value.astype(BF16)
            low = (value - high.astype(F32)).astype(BF16)
            left_side = lhs[2 * c + z]
            both = nt_dot(left_side, jnp.concatenate([high, low], axis=0))
            fields.append(both[:, 0:LANE] + both[:, LANE : 2 * LANE])
        return fields

    if not scatter:
        for c in range(Z // 2):
            out[2 * c], out[2 * c + 1] = planes(c)
        return

    def exchange(slot, src, dst, device):
        copy = pltpu.make_async_remote_copy(
            src_ref=src, dst_ref=dst, send_sem=rs_send.at[slot], recv_sem=rs_recv.at[slot],
            device_id=device, device_id_type=MESH,
        )
        copy.start()
        return copy

    core = []
    for i in range(2):
        for z, value in enumerate(planes(2 * (1 - py) + i)):
            field[i, z] = value.reshape(field.shape[2:])
        core.append(exchange(i, field.at[i], r0.at[i], (px, 1 - py)))
    def own_planes(i):
        values = planes(2 * py + i)
        core[i].wait()
        for z in range(2):
            a0[i, z] = values[z].reshape(field.shape[2:]) + r0[i, z]

    own_planes(0)
    step_a = exchange(2, a0.at[0, 0, :, :, 1 - xq], r1a, xdev)
    step_c = [
        exchange(3 + d, a0.at[0, 1, lax.rem(zq + d + 1, 4)], rz.at[d], zdevs[d]) for d in range(3)
    ]
    own_planes(1)
    step_b = exchange(6, a0.at[1, 0, :, 1 - yq], r1b, ydev)
    step_g = exchange(7, a0.at[1, 1, :, :, 1 - xq, 0:8], r1h.at[0], xdev)
    step_h = exchange(8, a0.at[1, 1, :, 1 - yq, :, 8:16], r1h.at[1], ydev)
    step_a.wait()
    a1a[...] = a0[0, 0, :, :, xq] + r1a[...]
    step_a = exchange(9, a1a.at[:, 1 - yq], r2a, ydev)
    step_b.wait()
    a1b[...] = a0[1, 0, :, yq] + r1b[...]
    step_b = exchange(10, a1b.at[:, 1 - xq], r2b, xdev)
    step_g.wait()
    a1h[0] = a0[1, 1, :, :, xq, 0:8] + r1h[0]
    step_g = exchange(11, a1h.at[0, :, 1 - yq], r2h.at[0], ydev)
    step_h.wait()
    a1h[1] = a0[1, 1, :, yq, :, 8:16] + r1h[1]
    step_h = exchange(12, a1h.at[1, :, 1 - xq], r2h.at[1], xdev)

    def last_step(k):
        return [
            exchange(15 + 3 * k + d, a2.at[k, lax.rem(zq + d + 1, 4)], r3.at[k, d], zdevs[d])
            for d in range(3)
        ]

    total = a0[0, 1, zq]
    for d, copy in enumerate(step_c):
        copy.wait()
        total = total + rz[d]
    c1[...] = total
    step_c = exchange(13, c1.at[:, 1 - xq], rcx, xdev)
    step_a.wait()
    a2[0] = a1a[:, yq] + r2a[...]
    ends = [last_step(0)]
    step_b.wait()
    a2[1] = a1b[:, xq] + r2b[...]
    ends.append(last_step(1))
    step_g.wait()
    a2[2, :, 0:8] = a1h[0, :, yq] + r2h[0]
    step_h.wait()
    a2[2, :, 8:16] = a1h[1, :, xq] + r2h[1]
    ends.append(last_step(2))
    step_c.wait()
    c2[...] = c1[:, xq] + rcx[...]
    step_c = exchange(14, c2.at[1 - yq], rcy, ydev)
    results = []
    for k in range(3):
        total = a2[k, zq]
        for d, copy in enumerate(ends[k]):
            copy.wait()
            total = total + r3[k, d]
        results.append(total)
    step_c.wait()
    results.insert(1, c2[yq] + rcy[...])
    first_half = lax.broadcasted_iota(jnp.int32, (share, LANE), 1) < 64
    for z, result in enumerate(results):
        reals, imags = [], []
        for j in range(2):
            even = result[2 * j * share : (2 * j + 1) * share]
            odd = result[(2 * j + 1) * share : (2 * j + 2) * share]
            reals.append(jnp.where(first_half, even, pltpu.roll(odd, 64, 1)))
            imags.append(jnp.where(first_half, pltpu.roll(even, 64, 1), odd))
        out[z] = jnp.concatenate(reals + imags, axis=1)


def on_device(
    levels, conv_table, conv_bias, mix_weight, mix_bias, decoder, green_rows, green_cols, focal_order
):
    npx = lax.axis_size("px")
    npy = lax.axis_size("py")
    nrows, ncols = levels.shape
    wide = ncols + LANE
    scatter = npx == 16 and npy == 2
    width = CH * V
    share = U // npx
    rows = green_rows.transpose(0, 1, 3, 2).reshape(Z * 2 * nrows, U)
    cols = green_cols.reshape(Z * 2 * V, ncols)
    operands = (
        levels, conv_table, conv_bias.reshape(1, HID), mix_weight, mix_bias.reshape(1, HID),
        decoder, rows, cols, focal_order.reshape(1, U),
    )

    def rs(*shape):
        return pltpu.VMEM(shape if scatter else (8, LANE), F32)

    def like(array):
        return pltpu.VMEM(array.shape, array.dtype)

    result = pl.pallas_call(
        functools.partial(kernel, npx, npy, scatter),
        out_shape=jax.ShapeDtypeStruct((Z // npy, share, width) if scatter else (Z, 4 * U, 2 * V), F32),
        in_specs=[pl.BlockSpec(memory_space=pltpu.HBM)] * 9,
        out_specs=pl.BlockSpec(memory_space=pltpu.VMEM),
        scratch_shapes=[
            *[like(operands[i]) for i in (0, 1, 2, 3, 4, 5, 6, 8)],
            pltpu.VMEM((16, ncols), jnp.int32),
            pltpu.VMEM((32, LANE), jnp.int32),
            pltpu.VMEM((32, LANE), jnp.int32),
            pltpu.VMEM((3, 32, ncols), jnp.int32),
            pltpu.VMEM(((nrows + 2) * 3 * LEVELS, ncols), BF16),
            pltpu.VMEM((2 * HID, 192), F32),
            pltpu.VMEM((4 * HID, 4 * HID), F32),
            pltpu.VMEM((8 * KS * CH, 4 * HID), F32),
            pltpu.VMEM(((nrows + 2 * M) * KS * CH, ncols), F32),
            pltpu.VMEM(cols.shape, F32),
            pltpu.VMEM((8, cols.shape[0]), F32),
            pltpu.VMEM((8, cols.shape[0]), F32),
            pltpu.VMEM((cols.shape[0], wide), BF16),
            pltpu.VMEM((4 * Z, U), F32),
            pltpu.VMEM((4 * Z, U), F32),
            pltpu.VMEM((2, 4 * Z, U), F32),
            pltpu.VMEM((2, 8, cols.shape[0]), F32),
            pltpu.VMEM((wide, CH * 32), BF16),
            pltpu.VMEM((Z, 4 * U, 2 * LANE), BF16),
            rs(2, 2, 4, 2, 2, 16, LANE),
            rs(2, 2, 4, 2, 2, 16, LANE),
            rs(2, 2, 4, 2, 2, 16, LANE),
            rs(4, 2, 16, LANE),
            rs(4, 2, 16, LANE),
            rs(2, 4, 2, 8, LANE),
            rs(4, 2, 16, LANE),
            rs(4, 2, 16, LANE),
            rs(2, 4, 2, 8, LANE),
            rs(4, 16, LANE),
            rs(4, 16, LANE),
            rs(2, 4, 8, LANE),
            rs(3, 4, 16, LANE),
            rs(3, 3, 16, LANE),
            rs(3, 2, 2, 16, LANE),
            rs(2, 2, 16, LANE),
            rs(2, 16, LANE),
            rs(2, 16, LANE),
            rs(16, LANE),
            pltpu.SemaphoreType.DMA((12,)),
            pltpu.SemaphoreType.DMA((12,)),
            pltpu.SemaphoreType.DMA((24,)),
            pltpu.SemaphoreType.DMA((24,)),
            pltpu.SemaphoreType.DMA((9,)),
        ],
        compiler_params=pltpu.CompilerParams(
            collective_id=0, has_side_effects=True, vmem_limit_bytes=56 * 1024 * 1024
        ),
    )(*operands)
    if scatter:
        return result
    result = result.reshape(Z, npx, 4 * share, 2 * V).transpose(1, 0, 2, 3)
    own = lax.psum_scatter(
        result.reshape(npx * Z, 4 * share * 2 * V), ("px", "py"), scatter_dimension=0, tiled=True
    )
    own = own.reshape(Z // npy, CH // 2, share, 2, V).transpose(0, 2, 3, 1, 4)
    return own.reshape(Z // npy, share, width)


def solution(mesh):
    return jax.shard_map(
        on_device,
        mesh=mesh,
        in_specs=(
            P("px", "py"),
            P(),
            P(),
            P(),
            P(),
            P(),
            P(None, None, None, "px"),
            P(None, None, None, "py"),
            P(),
        ),
        out_specs=P("py", "px", None),
        check_vma=False,
    )
```
